32 devices in a mesh: slab: 8 (over z, y), tile: 4 (over x, core).
Axes of the slice: x: 2, y: 2, z: 4, core: 2. Of those that a mesh axis runs over, the one named last changes fastest.
Arguments:
- brdf_bins: bfloat16 [3, 40, 180, 2048], P(None, 'slab', None, 'tile'), may hold values from -6 to 6
- diffusion: float32 [3, 40, 180], replicated, may hold values from 0.01 to 0.08
- valid_mask: int32 [40, 180], P('slab'), may hold values 0 or 1
- tile_owner: int32 [10], replicated, may hold values from 0 to 3, as said below
Outputs:
- owned_tiles: float32 [24, 512, 512], P('tile', 'slab')
The draws below stay inside these ranges and needn't reach their ends.
Inputs may be any that keep to these rules, and one draw needn't show every extreme that they name: `tile_owner`: one owner holds exactly 6 tiles and none more; no owner holds more than 2 tiles of one tile row or of one tile column, and some owner holds 2 of some row and 2 of some column; counts are uneven.
All inputs are finite; a program needn't handle non-finite values. No bound on the sum of `valid_mask` on one device may be relied on, other than what follows from the above.
Results may differ from the reference program's by a relative error of at most 0.0003.
Values may be sent and summed in bfloat16 or wider, within the bound.
A program may use at most 128 MiB of HBM per device.

```python
import math
import jax
import jax.numpy as jnp
import numpy as np
from jax import lax

CH = 3
PD = 180
MAT_DEV = 512
SWEEPS = 2
TD = 40
MATERIALS = 2048
U = 10
CAP = 6
N_TILE = 4


def draw_brdf_bins(key, part):
    families = 32
    key_proto = jax.random.fold_in(key, 21)
    key_first = jax.random.fold_in(key, 22)
    key_second = jax.random.fold_in(key, 23)
    key_wfirst = jax.random.fold_in(key, 24)
    key_wsecond = jax.random.fold_in(key, 25)
    key_noise = jax.random.fold_in(key, 26)
    first = jax.random.randint(key_first, (MATERIALS,), 0, families)
    second = (first + 1 + jax.random.randint(key_second, (MATERIALS,), 0, families - 1)) % families
    weight_first = jax.random.uniform(key_wfirst, (MATERIALS,), jnp.float32, 0.5, 0.8)
    weight_second = jax.random.uniform(key_wsecond, (MATERIALS,), jnp.float32, 0.2, 0.5)
    proto = jax.random.normal(key_proto, (CH, TD, PD, families), jnp.float32)
    noise = jax.random.normal(key_noise, (CH, TD, PD, MATERIALS), jnp.float32)
    value = weight_first * jnp.take(proto, first, axis=-1) + weight_second * jnp.take(proto, second, axis=-1)
    value = value + 0.5 * noise
    return jnp.clip(value, -6.0, 6.0).astype(jnp.bfloat16)


def draw_tile_owner(key, part):
    key_busy = jax.random.fold_in(key, 11)
    key_shuffle = jax.random.fold_in(key, 12)
    key_pick = jax.random.fold_in(key, 13)
    key_rowsign = jax.random.fold_in(key, 14)
    key_colsign = jax.random.fold_in(key, 15)
    key_offset = jax.random.fold_in(key, 16)
    row_tile, col_tile = np.triu_indices(N_TILE)
    busiest = jax.random.randint(key_busy, (), 0, N_TILE)
    others = (busiest + 1 + jax.random.permutation(key_shuffle, N_TILE - 1)) % N_TILE
    row_sign = 2 * jax.random.randint(key_rowsign, (), 0, 2) - 1
    col_sign = 2 * jax.random.randint(key_colsign, (), 0, 2) - 1
    offset = jax.random.randint(key_offset, (), 0, N_TILE - 1)
    rows_j = jnp.asarray(row_tile.astype(np.int32))
    cols_j = jnp.asarray(col_tile.astype(np.int32))
    classes = (row_sign * rows_j + col_sign * cols_j + offset) % (N_TILE - 1)
    base = others[classes]
    band_list = [index for index in range(row_tile.shape[0]) if col_tile[index] - row_tile[index] <= 1]
    band_ids = np.asarray(band_list, dtype=np.int32)
    pick_order = jax.random.permutation(key_pick, band_ids.shape[0])
    picked = jnp.asarray(band_ids)[pick_order[:CAP]]
    owner = base.at[picked].set(busiest)
    top_label = N_TILE - 1
    top_present = jnp.any(owner == top_label)
    swapped = jnp.where(owner == busiest, top_label, jnp.where(owner == top_label, busiest, owner))
    owner = jnp.where(top_present, owner, swapped)
    return owner.astype(jnp.int32)


def place_ends(values, rng, least, high):
    place = [jax.random.randint(jax.random.fold_in(rng, axis), (), 0, length) for axis, length in enumerate(values.shape)]
    longest = values.shape.index(max(values.shape))
    next_to = place[:longest] + [(place[longest] + 1) % values.shape[longest]] + place[longest + 1:]
    return values.at[tuple(place)].set(least).at[tuple(next_to)].set(high)


def setup_inputs(seed: int = 0) -> dict:
    keys = jax.random.split(jax.random.key(seed), 5)
    brdf_bins = draw_brdf_bins(jax.random.fold_in(keys[4], 71), 0)
    diffusion = jnp.clip(jnp.exp(jax.random.uniform(keys[1], (CH, TD, PD), jnp.float32, math.log(0.01), math.log(0.08))), 0.01, 0.08)
    valid_mask = place_ends((jax.random.randint(keys[2], (TD, PD), 0, 4) < 3).astype(jnp.int32), jax.random.fold_in(keys[2], 1), 0, 1)
    tile_owner = draw_tile_owner(jax.random.fold_in(keys[4], 71), 0)
    return {"brdf_bins": brdf_bins, "diffusion": diffusion, "valid_mask": valid_mask, "tile_owner": tile_owner}


def sweep_once(field, diffusion):
    pad_theta = jnp.pad(field, ((0, 0), (1, 1), (0, 0), (0, 0)))
    pad_chan = jnp.pad(field, ((1, 1), (0, 0), (0, 0), (0, 0)))
    neighbours = pad_theta[:, 2:] + pad_theta[:, :-2] + pad_chan[2:] + pad_chan[:-2]
    neighbours = neighbours + jnp.roll(field, 1, 2) + jnp.roll(field, -1, 2)
    return field + diffusion[..., None] * (neighbours - 6.0 * field)

def reference(brdf_bins, diffusion, valid_mask, tile_owner):
    field = brdf_bins.astype(jnp.float32)
    for sweep_idx in range(SWEEPS):
        field = sweep_once(field, diffusion)
    smooth = (field * valid_mask[None, :, :, None].astype(jnp.float32)).astype(jnp.bfloat16)
    flat_rows = smooth.reshape(-1, smooth.shape[-1])
    gram_scale = 1.0 / math.sqrt(flat_rows.shape[0])
    gram_full = jnp.dot(flat_rows.T, flat_rows, preferred_element_type=jnp.float32) * gram_scale
    row_tile, col_tile = np.triu_indices(N_TILE)
    blocks = gram_full.reshape(N_TILE, MAT_DEV, N_TILE, MAT_DEV).transpose(0, 2, 1, 3)
    upper_tiles = blocks[row_tile, col_tile]
    position = jnp.arange(U, dtype=jnp.int32)
    before = (tile_owner[None, :] == tile_owner[:, None]) & (position[None, :] < position[:, None])
    rank_in = lax.optimization_barrier(jnp.sum(before.astype(jnp.int32), axis=1))
    target = (tile_owner * CAP + rank_in).astype(jnp.int32)
    owned = jnp.zeros((N_TILE * CAP, MAT_DEV, MAT_DEV), jnp.float32)
    return owned.at[target].set(upper_tiles)
```

```python
import functools
import math

import jax
import jax.numpy as jnp
import numpy as np
from jax import lax
from jax.experimental import pallas as pl
from jax.experimental.pallas import tpu as pltpu
from jax.sharding import PartitionSpec as P

SWEEPS = 2


def padded_2(cells, sides, width):
    for axis, dim in sides:
        count = lax.axis_size(axis)
        ends = count - 1
        head = lax.slice_in_dim(cells, 0, width, axis=dim)
        tail = lax.slice_in_dim(cells, cells.shape[dim] - width, cells.shape[dim], axis=dim)
        cells = jnp.concatenate(
            [
                lax.ppermute(tail, axis, [(i, (i + 1) % count) for i in range(ends)]),
                cells,
                lax.ppermute(head, axis, [((i + 1) % count, i) for i in range(ends)]),
            ],
            axis=dim,
        )
    return cells


def stencil(padded, diffusion_rows):
    center = padded[:, 1:-1]
    pad_chan = jnp.pad(center, ((1, 1), (0, 0), (0, 0), (0, 0)))
    neighbours = padded[:, 2:] + padded[:, :-2] + pad_chan[2:] + pad_chan[:-2]
    neighbours = neighbours + jnp.roll(center, 1, 2) + jnp.roll(center, -1, 2)
    return center + diffusion_rows[..., None] * (neighbours - 6.0 * center)


def contract_rows(left_cols, right_cols):
    return lax.dot_general(
        left_cols, right_cols, (((0,), (0,)), ((), ())), preferred_element_type=jnp.float32
    )


def on_device(brdf_bins, diffusion, valid_mask, tile_owner):
    n_tiles = lax.axis_size("tile")
    my_tile = lax.axis_index("tile")
    slab_width = brdf_bins.shape[1]
    slab_start = lax.axis_index("slab") * slab_width
    extended = padded_2(brdf_bins, (("slab", 1),), SWEEPS)
    field = extended.astype(jnp.float32)
    margin_diffusion = jnp.pad(diffusion, ((0, 0), (SWEEPS - 1, SWEEPS - 1), (0, 0)))
    for sweep_idx in range(SWEEPS):
        span_rows = slab_width + 2 * (SWEEPS - 1 - sweep_idx)
        local_diffusion = lax.dynamic_slice_in_dim(
            margin_diffusion, slab_start + sweep_idx, span_rows, 1
        )
        field = stencil(field, local_diffusion)
    smooth = (field * valid_mask[None, :, :, None].astype(jnp.float32)).astype(jnp.bfloat16)
    flat_rows = smooth.reshape(-1, smooth.shape[-1])
    tile_width = flat_rows.shape[1]
    gram_scale = 1.0 / math.sqrt(flat_rows.shape[0] * lax.axis_size("slab"))
    row_tile, col_tile = np.triu_indices(n_tiles)
    n_upper = row_tile.shape[0]
    column_block = contract_rows(lax.all_gather(flat_rows, "tile", axis=1, tiled=True), flat_rows)
    tile_slots = column_block.reshape(n_tiles, tile_width, tile_width)
    slot_table = np.full((n_tiles, n_tiles), -1, np.int32)
    slot_table[col_tile, row_tile] = np.arange(n_upper, dtype=np.int32)
    reduced = lax.psum_scatter(tile_slots, "slab", scatter_dimension=1, tiled=True) * gram_scale
    my_upper = jnp.asarray(slot_table)[my_tile]
    has_upper = my_upper >= 0
    safe_upper = jnp.clip(my_upper, 0, n_upper - 1)
    destination = jnp.where(has_upper, tile_owner[safe_upper], -1)
    position = jnp.arange(n_upper, dtype=jnp.int32)
    same_owner = tile_owner[None, :] == tile_owner[:, None]
    before = same_owner & (position[None, :] < position[:, None])
    rank_in = jnp.sum(before.astype(jnp.int32), axis=1)
    to_dest = (destination[None, :] == jnp.arange(n_tiles, dtype=jnp.int32)[:, None]).astype(
        jnp.float32
    )
    outgoing = to_dest[:, :, None, None] * reduced[None]
    received = lax.all_to_all(outgoing, "tile", split_axis=0, concat_axis=0, tiled=True)
    received = received.reshape(n_tiles * n_tiles, received.shape[2], received.shape[3])
    recv_index = jnp.asarray((col_tile * n_tiles + row_tile).astype(np.int32))
    cap_slots = 2 * ((n_upper + n_tiles - 1) // n_tiles)
    slot_ids = jnp.arange(cap_slots, dtype=jnp.int32)
    chosen = (tile_owner[None, :] == my_tile) & (rank_in[None, :] == slot_ids[:, None])
    source_idx = jnp.sum(jnp.where(chosen, recv_index[None, :], 0), axis=1).astype(jnp.int32)
    filled = jnp.any(chosen, axis=1)
    picked = jnp.take(received, source_idx, axis=0)
    return jnp.where(filled[:, None, None], picked, 0.0)


MESH = pl.DeviceIdType.MESH
LANES = 128
HALF = 96
OFF = 8
SEGS = ((0, 512), (512, 256), (768, 512), (1280, 512))


def contract(left, right):
    return lax.dot_general(
        left, right, (((0,), (0,)), ((), ())), preferred_element_type=jnp.float32
    )


def gram_kernel(
    scale, bins, diff, mask, out, lo, hi, f0, f1, smooth, partner, across, gram, ybuf, zbuf,
    halo_send, halo_recv, core_send, core_recv, x_send, x_recv, y_send, y_recv, z_send, z_recv,
    g_send, g_recv, gx_send, gx_recv, gf_send, gf_recv,
):
    slab = lax.axis_index("slab")
    tile = lax.axis_index("tile")
    z = slab // 2
    y = lax.rem(slab, 2)
    chip = tile // 2
    core = lax.rem(tile, 2)
    core_peer = 2 * chip + 1 - core
    x_peer = lax.rem(tile + 2, 4)
    chans, rows, phis, width = bins.shape
    n_chunk = width // LANES
    groups = chans * rows
    half_rows = groups * HALF

    barrier = pltpu.get_barrier_semaphore()
    for step in range(1, 8):
        pl.semaphore_signal(
            barrier, inc=1, device_id=(lax.rem(slab + step, 8), tile), device_id_type=MESH
        )
    for other in (core_peer, x_peer):
        pl.semaphore_signal(barrier, inc=1, device_id=(slab, other), device_id_type=MESH)
    pl.semaphore_wait(barrier, 9)

    def lanes_of(m):
        return pl.ds(pl.multiple_of(m * LANES, LANES), LANES)

    def halo_up(m):
        return pltpu.make_async_remote_copy(
            src_ref=bins.at[:, pl.ds(rows - 2, 2), :, lanes_of(m)],
            dst_ref=lo.at[:, :, :, lanes_of(m)],
            send_sem=halo_send.at[0, m], recv_sem=halo_recv.at[0, m],
            device_id=(jnp.minimum(slab + 1, 7), tile), device_id_type=MESH,
        )

    def halo_down(m):
        return pltpu.make_async_remote_copy(
            src_ref=bins.at[:, pl.ds(0, 2), :, lanes_of(m)],
            dst_ref=hi.at[:, :, :, lanes_of(m)],
            send_sem=halo_send.at[1, m], recv_sem=halo_recv.at[1, m],
            device_id=(jnp.maximum(slab - 1, 0), tile), device_id_type=MESH,
        )

    for m in range(n_chunk):
        @pl.when(slab < 7)
        def _():
            halo_up(m).start()

        @pl.when(slab > 0)
        def _():
            halo_down(m).start()

    @pl.when(slab == 0)
    def _():
        lo[...] = jnp.zeros_like(lo)

    @pl.when(slab == 7)
    def _():
        hi[...] = jnp.zeros_like(hi)

    for ref in (f0, f1):
        for c in range(ref.shape[0]):
            for t in range(ref.shape[1]):
                ref[c, t, 184:208, :] = jnp.zeros((24, LANES), jnp.float32)

    def core_copy(m):
        return pltpu.make_async_remote_copy(
            src_ref=smooth.at[:, lanes_of(m)], dst_ref=partner.at[:, lanes_of(m)],
            send_sem=core_send.at[m], recv_sem=core_recv.at[m],
            device_id=(slab, core_peer), device_id_type=MESH,
        )

    def x_copy(m):
        start = pl.multiple_of((1 - chip) * half_rows, HALF)
        return pltpu.make_async_remote_copy(
            src_ref=smooth.at[pl.ds(start, half_rows), lanes_of(m)],
            dst_ref=across.at[:, lanes_of(m)],
            send_sem=x_send.at[m], recv_sem=x_recv.at[m],
            device_id=(slab, x_peer), device_id_type=MESH,
        )

    def sweep(ref, c, e, r, coef):
        here = ref[c, e, pl.ds(OFF + r, HALF), :]
        near = ref[c, e + 1, pl.ds(OFF + r, HALF), :] + ref[c, e - 1, pl.ds(OFF + r, HALF), :]
        if c + 1 < chans:
            near = near + ref[c + 1, e, pl.ds(OFF + r, HALF), :]
        if c > 0:
            near = near + ref[c - 1, e, pl.ds(OFF + r, HALF), :]
        near = near + ref[c, e, pl.ds(OFF + r - 1, HALF), :]
        near = near + ref[c, e, pl.ds(OFF + r + 1, HALF), :]
        return here + coef * (near - 6.0 * here)

    def chunk(m, carry):
        @pl.when(slab > 0)
        def _():
            halo_up(m).wait_recv()

        @pl.when(slab < 7)
        def _():
            halo_down(m).wait_recv()

        lanes = lanes_of(m)
        for c in range(chans):
            for e in range(rows + 4):
                if e < 2:
                    block = lo[c, e, :, lanes]
                elif e < rows + 2:
                    block = bins[c, e - 2, :, lanes]
                else:
                    block = hi[c, e - rows - 2, :, lanes]
                block = block.astype(jnp.float32)
                f0[c, e, OFF:OFF + phis, :] = block
                f0[c, e, OFF - 1:OFF, :] = block[phis - 1:phis]
                f0[c, e, OFF + phis:OFF + phis + 1, :] = block[0:1]

        def first(t, carry):
            for c in range(chans):
                for r in (0, HALF):
                    f1[c, t, pl.ds(OFF + r, HALF), :] = sweep(
                        f0, c, t + 1, r, diff[c, t, pl.ds(r, HALF), :]
                    )
                f1[c, t, OFF - 1:OFF, :] = f1[c, t, OFF + phis - 1:OFF + phis, :]
                f1[c, t, OFF + phis:OFF + phis + 1, :] = f1[c, t, OFF:OFF + 1, :]
            return carry

        lax.fori_loop(0, rows + 2, first, 0)

        def second(t, carry):
            for c in range(chans):
                for h in range(2):
                    r = h * HALF
                    value = sweep(f1, c, t + 1, r, diff[c, t + 1, pl.ds(r, HALF), :])
                    value = value * mask[t, pl.ds(r, HALF), :]
                    at = pl.multiple_of(h * half_rows + (c * rows + t) * HALF, HALF)
                    smooth[pl.ds(at, HALF), lanes] = value.astype(jnp.bfloat16)
            return carry

        lax.fori_loop(0, rows, second, 0)
        core_copy(m).start()
        x_copy(m).start()
        return carry

    lax.fori_loop(0, n_chunk, chunk, 0)

    def y_copy(k, zz):
        at, size = SEGS[k]
        return pltpu.make_async_remote_copy(
            src_ref=gram.at[pl.ds(pl.multiple_of((2 * zz + 1 - y) * 64, 64), 64), pl.ds(at, size)],
            dst_ref=ybuf.at[pl.ds(zz * 64, 64), pl.ds(at, size)],
            send_sem=y_send.at[k, zz], recv_sem=y_recv.at[k, zz],
            device_id=(2 * z + 1 - y, tile), device_id_type=MESH,
        )

    def z_copy(k, step):
        at, size = SEGS[k]
        zz = lax.rem(z + step, 4)
        return pltpu.make_async_remote_copy(
            src_ref=gram.at[pl.ds(pl.multiple_of((2 * zz + y) * 64, 64), 64), pl.ds(at, size)],
            dst_ref=zbuf.at[step - 1, :, pl.ds(at, size)],
            send_sem=z_send.at[k, step - 1], recv_sem=z_recv.at[k, step - 1],
            device_id=(2 * zz + y, tile), device_id_type=MESH,
        )

    def gather_copy(k, peer, send, recv):
        at, size = SEGS[k]
        return pltpu.make_async_remote_copy(
            src_ref=out.at[tile, :, pl.ds(at, size)], dst_ref=out.at[tile, :, pl.ds(at, size)],
            send_sem=send.at[k], recv_sem=recv.at[k],
            device_id=(slab, peer), device_id_type=MESH,
        )

    def forward_copy(k):
        at, size = SEGS[k]
        return pltpu.make_async_remote_copy(
            src_ref=out.at[x_peer, :, pl.ds(at, size)], dst_ref=out.at[x_peer, :, pl.ds(at, size)],
            send_sem=gf_send.at[k], recv_sem=gf_recv.at[k],
            device_id=(slab, core_peer), device_id_type=MESH,
        )

    def y_start(k):
        for zz in range(4):
            y_copy(k, zz).start()

    def y_finish(k):
        at, size = SEGS[k]
        for zz in (0, 1, 2, 3):
            y_copy(k, zz).wait_recv()
        for zz in range(4):
            mine = pl.ds(pl.multiple_of((2 * zz + y) * 64, 64), 64)
            gram[mine, pl.ds(at, size)] += ybuf[pl.ds(zz * 64, 64), pl.ds(at, size)]
        for step in (2, 1, 3):
            z_copy(k, step).start()

    def z_finish(k):
        at, size = SEGS[k]
        for step in (1, 2, 3):
            z_copy(k, step).wait_recv()
        cols = pl.ds(at, size)
        total = gram[pl.ds(pl.multiple_of(slab * 64, 64), 64), cols]
        for step in range(3):
            total = total + zbuf[step, :, cols]
        out[tile, :, cols] = total * scale
        gather_copy(k, x_peer, gx_send, gx_recv).start()
        gather_copy(k, core_peer, g_send, g_recv).start()

    def pair(left, right, at):
        gram[:, at:at + right.shape[1]] = contract(left[...], right[...])

    def half_of(ref, h):
        return ref.at[h * half_rows:(h + 1) * half_rows, :]

    own = slice(0, 512)
    gram[:, own] = contract(half_of(smooth, 0)[...], half_of(smooth, 0)[...])
    gram[:, own] += contract(half_of(smooth, 1)[...], half_of(smooth, 1)[...])
    y_start(0)
    for m in range(n_chunk):
        core_copy(m).wait_recv()
    for c in range(2):
        left, right = (smooth, partner) if c == 0 else (partner, smooth)

        @pl.when(core == c)
        def _():
            cols = slice(c * 256, c * 256 + 256)
            gram[:, 512:768] = contract(left[0:half_rows, :], right[0:half_rows, cols])
            gram[:, 512:768] += contract(left[half_rows:, :], right[half_rows:, cols])
    y_start(1)
    for m in range(n_chunk):
        x_copy(m).wait_recv()
    for piece in range(2):
        for x in range(2):
            for c in range(2):
                mine = smooth if piece == c else partner

                @pl.when(tile == 2 * x + c)
                def _():
                    if x == 0:
                        pair(half_of(mine, 0), across, 768 + 512 * piece)
                    else:
                        pair(across, half_of(mine, 1), 768 + 512 * piece)
        y_start(2 + piece)
    for k in range(4):
        y_finish(k)
    for k in range(4):
        z_finish(k)
    for k in range(4):
        gather_copy(k, x_peer, gx_send, gx_recv).wait_recv()
        forward_copy(k).start()
    for k in range(4):
        gather_copy(k, core_peer, g_send, g_recv).wait_recv()
        forward_copy(k).wait_recv()

    for m in range(n_chunk):
        @pl.when(slab < 7)
        def _():
            halo_up(m).wait_send()

        @pl.when(slab > 0)
        def _():
            halo_down(m).wait_send()
        core_copy(m).wait_send()
        x_copy(m).wait_send()
    for k in range(4):
        for zz in range(4):
            y_copy(k, zz).wait_send()
        for step in (1, 2, 3):
            z_copy(k, step).wait_send()
        gather_copy(k, x_peer, gx_send, gx_recv).wait_send()
        gather_copy(k, core_peer, g_send, g_recv).wait_send()
        forward_copy(k).wait_send()


def fused(brdf_bins, diffusion, valid_mask, tile_owner):
    chans, rows, phis, width = brdf_bins.shape
    slab = lax.axis_index("slab")
    my_tile = lax.axis_index("tile")
    margin = jnp.pad(diffusion, ((0, 0), (1, 1), (0, 2 * HALF - phis)))
    local = lax.dynamic_slice_in_dim(margin, slab * rows, rows + 2, 1)
    diff = jnp.broadcast_to(local[..., None], local.shape + (LANES,))
    mask = jnp.pad(valid_mask.astype(jnp.float32), ((0, 0), (0, 2 * HALF - phis)))
    mask = jnp.broadcast_to(mask[..., None], mask.shape + (LANES,))
    scale = 1.0 / math.sqrt(chans * rows * phis * lax.axis_size("slab"))
    dma = pltpu.SemaphoreType.DMA
    all_rows = chans * rows * 2 * HALF
    parts = pl.pallas_call(
        functools.partial(gram_kernel, scale),
        out_shape=jax.ShapeDtypeStruct((4, 64, 1792), jnp.float32),
        in_specs=[pl.BlockSpec(memory_space=pltpu.VMEM)] * 3,
        out_specs=pl.BlockSpec(memory_space=pltpu.VMEM),
        scratch_shapes=[
            pltpu.VMEM((chans, 2, phis, width), jnp.bfloat16),
            pltpu.VMEM((chans, 2, phis, width), jnp.bfloat16),
            pltpu.VMEM((chans, rows + 4, 208, LANES), jnp.float32),
            pltpu.VMEM((chans, rows + 2, 208, LANES), jnp.float32),
            pltpu.VMEM((all_rows, width), jnp.bfloat16),
            pltpu.VMEM((all_rows, width), jnp.bfloat16),
            pltpu.VMEM((all_rows // 2, width), jnp.bfloat16),
            pltpu.VMEM((512, 1792), jnp.float32),
            pltpu.VMEM((256, 1792), jnp.float32),
            pltpu.VMEM((3, 64, 1792), jnp.float32),
            dma((2, 4)), dma((2, 4)), dma((4,)), dma((4,)), dma((4,)), dma((4,)),
            dma((4, 4)), dma((4, 4)), dma((4, 3)), dma((4, 3)),
            dma((4,)), dma((4,)), dma((4,)), dma((4,)), dma((4,)), dma((4,)),
        ],
        compiler_params=pltpu.CompilerParams(
            collective_id=0, has_side_effects=True, vmem_limit_bytes=48 * 1024 * 1024
        ),
    )(brdf_bins, diff, mask)
    own = [parts[t, :, 0:512] for t in range(4)]
    side = [parts[t, :, 512:768] for t in range(4)]
    cross = [[parts[t, :, 768 + 512 * p:1280 + 512 * p] for p in range(2)] for t in range(4)]
    row_tile, col_tile = np.triu_indices(4)
    tiles = []
    for i, j in zip(row_tile.tolist(), col_tile.tolist()):
        if i == j:
            tiles.append(own[i])
        elif i // 2 == j // 2:
            tiles.append(jnp.concatenate([side[i], side[j]], axis=1))
        else:
            tiles.append(cross[j - 2][i] + cross[2 + i][j - 2])
    tiles = jnp.stack(tiles)
    n_upper = len(row_tile)
    position = jnp.arange(n_upper, dtype=jnp.int32)
    before = (tile_owner[None, :] == tile_owner[:, None]) & (position[None, :] < position[:, None])
    rank_in = jnp.sum(before.astype(jnp.int32), axis=1)
    cap_slots = 2 * ((n_upper + 3) // 4)
    slot_ids = jnp.arange(cap_slots, dtype=jnp.int32)
    chosen = (tile_owner[None, :] == my_tile) & (rank_in[None, :] == slot_ids[:, None])
    source = jnp.sum(jnp.where(chosen, position[None, :], 0), axis=1).astype(jnp.int32)
    picked = jnp.take(tiles, source, axis=0)
    return jnp.where(jnp.any(chosen, axis=1)[:, None, None], picked, 0.0)


def solution(mesh):
    body = fused if (mesh.shape["slab"], mesh.shape["tile"]) == (8, 4) else on_device
    in_specs = (P(None, "slab", None, "tile"), P(), P("slab", None), P())
    out_specs = P("tile", "slab", None)
    return jax.shard_map(
        body, mesh=mesh, in_specs=in_specs, out_specs=out_specs, check_vma=False
    )
```

```python
import functools
import math

import jax
import jax.numpy as jnp
import numpy as np
from jax import lax
from jax.experimental import pallas as pl
from jax.experimental.pallas import tpu as pltpu
from jax.sharding import PartitionSpec as P

SWEEPS = 2


def padded_2(cells, sides, width):
    for axis, dim in sides:
        count = lax.axis_size(axis)
        ends = count - 1
        head = lax.slice_in_dim(cells, 0, width, axis=dim)
        tail = lax.slice_in_dim(cells, cells.shape[dim] - width, cells.shape[dim], axis=dim)
        cells = jnp.concatenate(
            [
                lax.ppermute(tail, axis, [(i, (i + 1) % count) for i in range(ends)]),
                cells,
                lax.ppermute(head, axis, [((i + 1) % count, i) for i in range(ends)]),
            ],
            axis=dim,
        )
    return cells


def stencil(padded, diffusion_rows):
    center = padded[:, 1:-1]
    pad_chan = jnp.pad(center, ((1, 1), (0, 0), (0, 0), (0, 0)))
    neighbours = padded[:, 2:] + padded[:, :-2] + pad_chan[2:] + pad_chan[:-2]
    neighbours = neighbours + jnp.roll(center, 1, 2) + jnp.roll(center, -1, 2)
    return center + diffusion_rows[..., None] * (neighbours - 6.0 * center)


def contract_rows(left_cols, right_cols):
    return lax.dot_general(
        left_cols, right_cols, (((0,), (0,)), ((), ())), preferred_element_type=jnp.float32
    )


def on_device(brdf_bins, diffusion, valid_mask, tile_owner):
    n_tiles = lax.axis_size("tile")
    my_tile = lax.axis_index("tile")
    slab_width = brdf_bins.shape[1]
    slab_start = lax.axis_index("slab") * slab_width
    extended = padded_2(brdf_bins, (("slab", 1),), SWEEPS)
    field = extended.astype(jnp.float32)
    margin_diffusion = jnp.pad(diffusion, ((0, 0), (SWEEPS - 1, SWEEPS - 1), (0, 0)))
    for sweep_idx in range(SWEEPS):
        span_rows = slab_width + 2 * (SWEEPS - 1 - sweep_idx)
        local_diffusion = lax.dynamic_slice_in_dim(
            margin_diffusion, slab_start + sweep_idx, span_rows, 1
        )
        field = stencil(field, local_diffusion)
    smooth = (field * valid_mask[None, :, :, None].astype(jnp.float32)).astype(jnp.bfloat16)
    flat_rows = smooth.reshape(-1, smooth.shape[-1])
    tile_width = flat_rows.shape[1]
    gram_scale = 1.0 / math.sqrt(flat_rows.shape[0] * lax.axis_size("slab"))
    row_tile, col_tile = np.triu_indices(n_tiles)
    n_upper = row_tile.shape[0]
    column_block = contract_rows(lax.all_gather(flat_rows, "tile", axis=1, tiled=True), flat_rows)
    tile_slots = column_block.reshape(n_tiles, tile_width, tile_width)
    slot_table = np.full((n_tiles, n_tiles), -1, np.int32)
    slot_table[col_tile, row_tile] = np.arange(n_upper, dtype=np.int32)
    reduced = lax.psum_scatter(tile_slots, "slab", scatter_dimension=1, tiled=True) * gram_scale
    my_upper = jnp.asarray(slot_table)[my_tile]
    has_upper = my_upper >= 0
    safe_upper = jnp.clip(my_upper, 0, n_upper - 1)
    destination = jnp.where(has_upper, tile_owner[safe_upper], -1)
    position = jnp.arange(n_upper, dtype=jnp.int32)
    same_owner = tile_owner[None, :] == tile_owner[:, None]
    before = same_owner & (position[None, :] < position[:, None])
    rank_in = jnp.sum(before.astype(jnp.int32), axis=1)
    to_dest = (destination[None, :] == jnp.arange(n_tiles, dtype=jnp.int32)[:, None]).astype(
        jnp.float32
    )
    outgoing = to_dest[:, :, None, None] * reduced[None]
    received = lax.all_to_all(outgoing, "tile", split_axis=0, concat_axis=0, tiled=True)
    received = received.reshape(n_tiles * n_tiles, received.shape[2], received.shape[3])
    recv_index = jnp.asarray((col_tile * n_tiles + row_tile).astype(np.int32))
    cap_slots = 2 * ((n_upper + n_tiles - 1) // n_tiles)
    slot_ids = jnp.arange(cap_slots, dtype=jnp.int32)
    chosen = (tile_owner[None, :] == my_tile) & (rank_in[None, :] == slot_ids[:, None])
    source_idx = jnp.sum(jnp.where(chosen, recv_index[None, :], 0), axis=1).astype(jnp.int32)
    filled = jnp.any(chosen, axis=1)
    picked = jnp.take(received, source_idx, axis=0)
    return jnp.where(filled[:, None, None], picked, 0.0)


MESH = pl.DeviceIdType.MESH
LANES = 128
HALF = 96
OFF = 8
DEPTH = 2
LEVELS = 32767.0
SEGS = ((0, 512), (512, 256), (768, 512), (1280, 512))


def contract(left, right):
    return lax.dot_general(
        left, right, (((0,), (0,)), ((), ())), preferred_element_type=jnp.float32
    )


def coded(block):
    peak = jnp.maximum(jnp.max(jnp.abs(block), axis=0, keepdims=True), 1e-30)
    code = jnp.round(block * (LEVELS / peak)).astype(jnp.int32).astype(jnp.int16)
    return code, peak * (1.0 / LEVELS)


def decoded(code, unit):
    return code.astype(jnp.int32).astype(jnp.float32) * unit


def gram_kernel(
    scale, bins, diff, mask, out, lo, hi, f0, f1, smooth, partner, across, gram,
    yout, ybuf, youtu, ybufu, zout, zbuf, zoutu, zbufu,
    halo_send, halo_recv, core_send, core_recv, x_send, x_recv, y_send, y_recv, yu_send, yu_recv,
    z_send, z_recv, zu_send, zu_recv,
    g_send, g_recv, gx_send, gx_recv, gf_send, gf_recv,
):
    slab = lax.axis_index("slab")
    tile = lax.axis_index("tile")
    z = slab // 2
    y = lax.rem(slab, 2)
    chip = tile // 2
    core = lax.rem(tile, 2)
    core_peer = 2 * chip + 1 - core
    x_peer = lax.rem(tile + 2, 4)
    chans, rows, phis, width = bins.shape
    n_chunk = width // LANES
    groups = chans * rows
    half_rows = groups * HALF

    barrier = pltpu.get_barrier_semaphore()
    for step in range(1, 8):
        pl.semaphore_signal(
            barrier, inc=1, device_id=(lax.rem(slab + step, 8), tile), device_id_type=MESH
        )
    for other in (core_peer, x_peer):
        pl.semaphore_signal(barrier, inc=1, device_id=(slab, other), device_id_type=MESH)
    pl.semaphore_wait(barrier, 9)

    def lanes_of(m):
        return pl.ds(pl.multiple_of(m * LANES, LANES), LANES)

    def halo_up(m):
        return pltpu.make_async_remote_copy(
            src_ref=bins.at[:, pl.ds(rows - 2, 2), :, lanes_of(m)],
            dst_ref=lo.at[:, :, :, lanes_of(m)],
            send_sem=halo_send.at[0, m], recv_sem=halo_recv.at[0, m],
            device_id=(jnp.minimum(slab + 1, 7), tile), device_id_type=MESH,
        )

    def halo_down(m):
        return pltpu.make_async_remote_copy(
            src_ref=bins.at[:, pl.ds(0, 2), :, lanes_of(m)],
            dst_ref=hi.at[:, :, :, lanes_of(m)],
            send_sem=halo_send.at[1, m], recv_sem=halo_recv.at[1, m],
            device_id=(jnp.maximum(slab - 1, 0), tile), device_id_type=MESH,
        )

    def halo_start(m):
        @pl.when(slab < 7)
        def _():
            halo_up(m).start()

        @pl.when(slab > 0)
        def _():
            halo_down(m).start()

    for m in range(DEPTH):
        halo_start(m)

    @pl.when(slab == 0)
    def _():
        lo[...] = jnp.zeros_like(lo)

    @pl.when(slab == 7)
    def _():
        hi[...] = jnp.zeros_like(hi)

    for ref in (f0, f1):
        for c in range(ref.shape[0]):
            for t in range(ref.shape[1]):
                ref[c, t, 184:208, :] = jnp.zeros((24, LANES), jnp.float32)

    def core_copy(m):
        return pltpu.make_async_remote_copy(
            src_ref=smooth.at[:, lanes_of(m)], dst_ref=partner.at[:, lanes_of(m)],
            send_sem=core_send.at[m], recv_sem=core_recv.at[m],
            device_id=(slab, core_peer), device_id_type=MESH,
        )

    def x_copy(m):
        start = pl.multiple_of((1 - chip) * half_rows, HALF)
        return pltpu.make_async_remote_copy(
            src_ref=smooth.at[pl.ds(start, half_rows), lanes_of(m)],
            dst_ref=across.at[:, lanes_of(m)],
            send_sem=x_send.at[m], recv_sem=x_recv.at[m],
            device_id=(slab, x_peer), device_id_type=MESH,
        )

    def sweep(ref, c, e, r, coef):
        here = ref[c, e, pl.ds(OFF + r, HALF), :]
        near = ref[c, e + 1, pl.ds(OFF + r, HALF), :] + ref[c, e - 1, pl.ds(OFF + r, HALF), :]
        if c + 1 < chans:
            near = near + ref[c + 1, e, pl.ds(OFF + r, HALF), :]
        if c > 0:
            near = near + ref[c - 1, e, pl.ds(OFF + r, HALF), :]
        near = near + ref[c, e, pl.ds(OFF + r - 1, HALF), :]
        near = near + ref[c, e, pl.ds(OFF + r + 1, HALF), :]
        return here + coef * (near - 6.0 * here)

    def chunk(m, carry):
        @pl.when(slab > 0)
        def _():
            halo_up(m).wait_recv()

        @pl.when(slab < 7)
        def _():
            halo_down(m).wait_recv()

        @pl.when(slab < 7)
        def _():
            halo_up(m).wait_send()

        @pl.when(slab > 0)
        def _():
            halo_down(m).wait_send()

        @pl.when(m + DEPTH < n_chunk)
        def _():
            halo_start(m + DEPTH)

        lanes = lanes_of(m)
        for c in range(chans):
            for e in range(rows + 4):
                if e < 2:
                    block = lo[c, e, :, lanes]
                elif e < rows + 2:
                    block = bins[c, e - 2, :, lanes]
                else:
                    block = hi[c, e - rows - 2, :, lanes]
                block = block.astype(jnp.float32)
                f0[c, e, OFF:OFF + phis, :] = block
                f0[c, e, OFF - 1:OFF, :] = block[phis - 1:phis]
                f0[c, e, OFF + phis:OFF + phis + 1, :] = block[0:1]

        def first(t, carry):
            for c in range(chans):
                for r in (0, HALF):
                    f1[c, t, pl.ds(OFF + r, HALF), :] = sweep(
                        f0, c, t + 1, r, diff[c, t, pl.ds(r, HALF), :]
                    )
                f1[c, t, OFF - 1:OFF, :] = f1[c, t, OFF + phis - 1:OFF + phis, :]
                f1[c, t, OFF + phis:OFF + phis + 1, :] = f1[c, t, OFF:OFF + 1, :]
            return carry

        lax.fori_loop(0, rows + 2, first, 0)

        def second(t, carry):
            for c in range(chans):
                for h in range(2):
                    r = h * HALF
                    value = sweep(f1, c, t + 1, r, diff[c, t + 1, pl.ds(r, HALF), :])
                    value = value * mask[t, pl.ds(r, HALF), :]
                    at = pl.multiple_of(h * half_rows + (c * rows + t) * HALF, HALF)
                    smooth[pl.ds(at, HALF), lanes] = value.astype(jnp.bfloat16)
            return carry

        lax.fori_loop(0, rows, second, 0)
        core_copy(m).start()
        x_copy(m).start()
        return carry

    lax.fori_loop(0, n_chunk, chunk, 0)

    def y_copies(k):
        at, size = SEGS[k]
        cols = pl.ds(at, size)
        return [
            pltpu.make_async_remote_copy(
                src_ref=src.at[:, cols] if src.ndim == 2 else src.at[:, :, cols],
                dst_ref=dst.at[:, cols] if src.ndim == 2 else dst.at[:, :, cols],
                send_sem=send.at[k], recv_sem=recv.at[k],
                device_id=(2 * z + 1 - y, tile), device_id_type=MESH,
            )
            for src, dst, send, recv in (
                (yout, ybuf, y_send, y_recv), (youtu, ybufu, yu_send, yu_recv)
            )
        ]

    def z_copies(k, step):
        at, size = SEGS[k]
        cols = pl.ds(at, size)
        zz = lax.rem(z + step, 4)
        return [
            pltpu.make_async_remote_copy(
                src_ref=src.at[step - 1, :, cols], dst_ref=dst.at[step - 1, :, cols],
                send_sem=send.at[k, step - 1], recv_sem=recv.at[k, step - 1],
                device_id=(2 * zz + y, tile), device_id_type=MESH,
            )
            for src, dst, send, recv in (
                (zout, zbuf, z_send, z_recv), (zoutu, zbufu, zu_send, zu_recv)
            )
        ]

    def gather_copy(k, peer, send, recv):
        at, size = SEGS[k]
        return pltpu.make_async_remote_copy(
            src_ref=out.at[tile, :, pl.ds(at, size)], dst_ref=out.at[tile, :, pl.ds(at, size)],
            send_sem=send.at[k], recv_sem=recv.at[k],
            device_id=(slab, peer), device_id_type=MESH,
        )

    def forward_copy(k):
        at, size = SEGS[k]
        return pltpu.make_async_remote_copy(
            src_ref=out.at[x_peer, :, pl.ds(at, size)], dst_ref=out.at[x_peer, :, pl.ds(at, size)],
            send_sem=gf_send.at[k], recv_sem=gf_recv.at[k],
            device_id=(slab, core_peer), device_id_type=MESH,
        )

    def gram_rows(block):
        return pl.ds(pl.multiple_of(block * 64, 64), 64)

    def y_start(k):
        at, size = SEGS[k]
        cols = pl.ds(at, size)
        for zz in range(4):
            code, unit = coded(gram[gram_rows(2 * zz + 1 - y), cols])
            yout[pl.ds(zz * 64, 64), cols] = code
            youtu[zz, :, cols] = unit
        for copy in y_copies(k):
            copy.start()

    def y_finish(k):
        at, size = SEGS[k]
        cols = pl.ds(at, size)
        for copy in y_copies(k):
            copy.wait_recv()
        for zz in range(4):
            gram[gram_rows(2 * zz + y), cols] += decoded(
                ybuf[pl.ds(zz * 64, 64), cols], ybufu[zz, :, cols]
            )
        for step in (2, 1, 3):
            code, unit = coded(gram[gram_rows(2 * lax.rem(z + step, 4) + y), cols])
            zout[step - 1, :, cols] = code
            zoutu[step - 1, :, cols] = unit
            for copy in z_copies(k, step):
                copy.start()

    def z_finish(k):
        at, size = SEGS[k]
        for step in (1, 2, 3):
            for copy in z_copies(k, step):
                copy.wait_recv()
        cols = pl.ds(at, size)
        total = gram[pl.ds(pl.multiple_of(slab * 64, 64), 64), cols]
        for step in range(3):
            total = total + decoded(zbuf[step, :, cols], zbufu[step, :, cols])
        out[tile, :, cols] = total * scale
        gather_copy(k, x_peer, gx_send, gx_recv).start()
        gather_copy(k, core_peer, g_send, g_recv).start()

    def pair(left, right, at):
        gram[:, at:at + right.shape[1]] = contract(left[...], right[...])

    def half_of(ref, h):
        return ref.at[h * half_rows:(h + 1) * half_rows, :]

    own = slice(0, 512)
    gram[:, own] = contract(half_of(smooth, 0)[...], half_of(smooth, 0)[...])
    gram[:, own] += contract(half_of(smooth, 1)[...], half_of(smooth, 1)[...])
    y_start(0)
    for m in range(n_chunk):
        core_copy(m).wait_recv()
    for c in range(2):
        left, right = (smooth, partner) if c == 0 else (partner, smooth)

        @pl.when(core == c)
        def _():
            cols = slice(c * 256, c * 256 + 256)
            gram[:, 512:768] = contract(left[0:half_rows, :], right[0:half_rows, cols])
            gram[:, 512:768] += contract(left[half_rows:, :], right[half_rows:, cols])
    y_start(1)
    for m in range(n_chunk):
        x_copy(m).wait_recv()
    for piece in range(2):
        for x in range(2):
            for c in range(2):
                mine = smooth if piece == c else partner

                @pl.when(tile == 2 * x + c)
                def _():
                    if x == 0:
                        pair(half_of(mine, 0), across, 768 + 512 * piece)
                    else:
                        pair(across, half_of(mine, 1), 768 + 512 * piece)
        y_start(2 + piece)
    for k in range(4):
        y_finish(k)
    for k in range(4):
        z_finish(k)
    for k in range(4):
        gather_copy(k, x_peer, gx_send, gx_recv).wait_recv()
        forward_copy(k).start()
    for k in range(4):
        gather_copy(k, core_peer, g_send, g_recv).wait_recv()
        forward_copy(k).wait_recv()

    for m in range(n_chunk):
        core_copy(m).wait_send()
        x_copy(m).wait_send()
    for k in range(4):
        for copy in y_copies(k):
            copy.wait_send()
        for step in (1, 2, 3):
            for copy in z_copies(k, step):
                copy.wait_send()
        gather_copy(k, x_peer, gx_send, gx_recv).wait_send()
        gather_copy(k, core_peer, g_send, g_recv).wait_send()
        forward_copy(k).wait_send()


def fused(brdf_bins, diffusion, valid_mask, tile_owner):
    chans, rows, phis, width = brdf_bins.shape
    slab = lax.axis_index("slab")
    my_tile = lax.axis_index("tile")
    margin = jnp.pad(diffusion, ((0, 0), (1, 1), (0, 2 * HALF - phis)))
    local = lax.dynamic_slice_in_dim(margin, slab * rows, rows + 2, 1)
    diff = jnp.broadcast_to(local[..., None], local.shape + (LANES,))
    mask = jnp.pad(valid_mask.astype(jnp.float32), ((0, 0), (0, 2 * HALF - phis)))
    mask = jnp.broadcast_to(mask[..., None], mask.shape + (LANES,))
    scale = 1.0 / math.sqrt(chans * rows * phis * lax.axis_size("slab"))
    dma = pltpu.SemaphoreType.DMA
    all_rows = chans * rows * 2 * HALF
    parts = pl.pallas_call(
        functools.partial(gram_kernel, scale),
        out_shape=jax.ShapeDtypeStruct((4, 64, 1792), jnp.float32),
        in_specs=[pl.BlockSpec(memory_space=pltpu.VMEM)] * 3,
        out_specs=pl.BlockSpec(memory_space=pltpu.VMEM),
        scratch_shapes=[
            pltpu.VMEM((chans, 2, phis, width), jnp.bfloat16),
            pltpu.VMEM((chans, 2, phis, width), jnp.bfloat16),
            pltpu.VMEM((chans, rows + 4, 208, LANES), jnp.float32),
            pltpu.VMEM((chans, rows + 2, 208, LANES), jnp.float32),
            pltpu.VMEM((all_rows, width), jnp.bfloat16),
            pltpu.VMEM((all_rows, width), jnp.bfloat16),
            pltpu.VMEM((all_rows // 2, width), jnp.bfloat16),
            pltpu.VMEM((512, 1792), jnp.float32),
            pltpu.VMEM((256, 1792), jnp.int16),
            pltpu.VMEM((256, 1792), jnp.int16),
            pltpu.VMEM((4, 1, 1792), jnp.float32),
            pltpu.VMEM((4, 1, 1792), jnp.float32),
            pltpu.VMEM((3, 64, 1792), jnp.int16),
            pltpu.VMEM((3, 64, 1792), jnp.int16),
            pltpu.VMEM((3, 1, 1792), jnp.float32),
            pltpu.VMEM((3, 1, 1792), jnp.float32),
            dma((2, 4)), dma((2, 4)), dma((4,)), dma((4,)), dma((4,)), dma((4,)),
            dma((4,)), dma((4,)), dma((4,)), dma((4,)),
            dma((4, 3)), dma((4, 3)), dma((4, 3)), dma((4, 3)),
            dma((4,)), dma((4,)), dma((4,)), dma((4,)), dma((4,)), dma((4,)),
        ],
        compiler_params=pltpu.CompilerParams(
            collective_id=0, has_side_effects=True, vmem_limit_bytes=48 * 1024 * 1024
        ),
    )(brdf_bins, diff, mask)
    own = [parts[t, :, 0:512] for t in range(4)]
    side = [parts[t, :, 512:768] for t in range(4)]
    cross = [[parts[t, :, 768 + 512 * p:1280 + 512 * p] for p in range(2)] for t in range(4)]
    row_tile, col_tile = np.triu_indices(4)
    tiles = []
    for i, j in zip(row_tile.tolist(), col_tile.tolist()):
        if i == j:
            tiles.append(own[i])
        elif i // 2 == j // 2:
            tiles.append(jnp.concatenate([side[i], side[j]], axis=1))
        else:
            tiles.append(cross[j - 2][i] + cross[2 + i][j - 2])
    tiles = jnp.stack(tiles)
    n_upper = len(row_tile)
    position = jnp.arange(n_upper, dtype=jnp.int32)
    before = (tile_owner[None, :] == tile_owner[:, None]) & (position[None, :] < position[:, None])
    rank_in = jnp.sum(before.astype(jnp.int32), axis=1)
    cap_slots = 2 * ((n_upper + 3) // 4)
    slot_ids = jnp.arange(cap_slots, dtype=jnp.int32)
    chosen = (tile_owner[None, :] == my_tile) & (rank_in[None, :] == slot_ids[:, None])
    source = jnp.sum(jnp.where(chosen, position[None, :], 0), axis=1).astype(jnp.int32)
    picked = jnp.take(tiles, source, axis=0)
    return jnp.where(jnp.any(chosen, axis=1)[:, None, None], picked, 0.0)


def solution(mesh):
    body = fused if (mesh.shape["slab"], mesh.shape["tile"]) == (8, 4) else on_device
    in_specs = (P(None, "slab", None, "tile"), P(), P("slab", None), P())
    out_specs = P("tile", "slab", None)
    return jax.shard_map(
        body, mesh=mesh, in_specs=in_specs, out_specs=out_specs, check_vma=False
    )
```

```python
import functools
import math

import jax
import jax.numpy as jnp
import numpy as np
from jax import lax
from jax.experimental import pallas as pl
from jax.experimental.pallas import tpu as pltpu
from jax.sharding import PartitionSpec as P

SWEEPS = 2


def padded_2(cells, sides, width):
    for axis, dim in sides:
        count = lax.axis_size(axis)
        ends = count - 1
        head = lax.slice_in_dim(cells, 0, width, axis=dim)
        tail = lax.slice_in_dim(cells, cells.shape[dim] - width, cells.shape[dim], axis=dim)
        cells = jnp.concatenate(
            [
                lax.ppermute(tail, axis, [(i, (i + 1) % count) for i in range(ends)]),
                cells,
                lax.ppermute(head, axis, [((i + 1) % count, i) for i in range(ends)]),
            ],
            axis=dim,
        )
    return cells


def stencil(padded, diffusion_rows):
    center = padded[:, 1:-1]
    pad_chan = jnp.pad(center, ((1, 1), (0, 0), (0, 0), (0, 0)))
    neighbours = padded[:, 2:] + padded[:, :-2] + pad_chan[2:] + pad_chan[:-2]
    neighbours = neighbours + jnp.roll(center, 1, 2) + jnp.roll(center, -1, 2)
    return center + diffusion_rows[..., None] * (neighbours - 6.0 * center)


def contract_rows(left_cols, right_cols):
    return lax.dot_general(
        left_cols, right_cols, (((0,), (0,)), ((), ())), preferred_element_type=jnp.float32
    )


def on_device(brdf_bins, diffusion, valid_mask, tile_owner):
    n_tiles = lax.axis_size("tile")
    my_tile = lax.axis_index("tile")
    slab_width = brdf_bins.shape[1]
    slab_start = lax.axis_index("slab") * slab_width
    extended = padded_2(brdf_bins, (("slab", 1),), SWEEPS)
    field = extended.astype(jnp.float32)
    margin_diffusion = jnp.pad(diffusion, ((0, 0), (SWEEPS - 1, SWEEPS - 1), (0, 0)))
    for sweep_idx in range(SWEEPS):
        span_rows = slab_width + 2 * (SWEEPS - 1 - sweep_idx)
        local_diffusion = lax.dynamic_slice_in_dim(
            margin_diffusion, slab_start + sweep_idx, span_rows, 1
        )
        field = stencil(field, local_diffusion)
    smooth = (field * valid_mask[None, :, :, None].astype(jnp.float32)).astype(jnp.bfloat16)
    flat_rows = smooth.reshape(-1, smooth.shape[-1])
    tile_width = flat_rows.shape[1]
    gram_scale = 1.0 / math.sqrt(flat_rows.shape[0] * lax.axis_size("slab"))
    row_tile, col_tile = np.triu_indices(n_tiles)
    n_upper = row_tile.shape[0]
    column_block = contract_rows(lax.all_gather(flat_rows, "tile", axis=1, tiled=True), flat_rows)
    tile_slots = column_block.reshape(n_tiles, tile_width, tile_width)
    slot_table = np.full((n_tiles, n_tiles), -1, np.int32)
    slot_table[col_tile, row_tile] = np.arange(n_upper, dtype=np.int32)
    reduced = lax.psum_scatter(tile_slots, "slab", scatter_dimension=1, tiled=True) * gram_scale
    my_upper = jnp.asarray(slot_table)[my_tile]
    has_upper = my_upper >= 0
    safe_upper = jnp.clip(my_upper, 0, n_upper - 1)
    destination = jnp.where(has_upper, tile_owner[safe_upper], -1)
    position = jnp.arange(n_upper, dtype=jnp.int32)
    same_owner = tile_owner[None, :] == tile_owner[:, None]
    before = same_owner & (position[None, :] < position[:, None])
    rank_in = jnp.sum(before.astype(jnp.int32), axis=1)
    to_dest = (destination[None, :] == jnp.arange(n_tiles, dtype=jnp.int32)[:, None]).astype(
        jnp.float32
    )
    outgoing = to_dest[:, :, None, None] * reduced[None]
    received = lax.all_to_all(outgoing, "tile", split_axis=0, concat_axis=0, tiled=True)
    received = received.reshape(n_tiles * n_tiles, received.shape[2], received.shape[3])
    recv_index = jnp.asarray((col_tile * n_tiles + row_tile).astype(np.int32))
    cap_slots = 2 * ((n_upper + n_tiles - 1) // n_tiles)
    slot_ids = jnp.arange(cap_slots, dtype=jnp.int32)
    chosen = (tile_owner[None, :] == my_tile) & (rank_in[None, :] == slot_ids[:, None])
    source_idx = jnp.sum(jnp.where(chosen, recv_index[None, :], 0), axis=1).astype(jnp.int32)
    filled = jnp.any(chosen, axis=1)
    picked = jnp.take(received, source_idx, axis=0)
    return jnp.where(filled[:, None, None], picked, 0.0)


MESH = pl.DeviceIdType.MESH
LANES = 128
HALF = 96
OFF = 8
DEPTH = 2
LEVELS = 32767.0
SEGS = ((0, 512), (512, 256), (768, 512), (1280, 512))


def contract(left, right):
    return lax.dot_general(
        left, right, (((0,), (0,)), ((), ())), preferred_element_type=jnp.float32
    )


def coded(block):
    peak = jnp.maximum(jnp.max(jnp.abs(block), axis=0, keepdims=True), 1e-30)
    code = jnp.round(block * (LEVELS / peak)).astype(jnp.int32).astype(jnp.int16)
    return code, peak * (1.0 / LEVELS)


def decoded(code, unit):
    return code.astype(jnp.int32).astype(jnp.float32) * unit


def gram_kernel(
    scale, bins, diff, mask, out, lo, hi, relay, f0, f1, smooth, partner, across, gram,
    yout, ybuf, youtu, ybufu, zout, zbuf, zoutu, zbufu,
    halo_send, halo_recv, relay_send, relay_recv, core_send, core_recv, x_send, x_recv, y_send, y_recv, yu_send, yu_recv,
    z_send, z_recv, zu_send, zu_recv,
    g_send, g_recv, gx_send, gx_recv, gf_send, gf_recv,
):
    slab = lax.axis_index("slab")
    tile = lax.axis_index("tile")
    z = slab // 2
    y = lax.rem(slab, 2)
    chip = tile // 2
    core = lax.rem(tile, 2)
    core_peer = 2 * chip + 1 - core
    x_peer = lax.rem(tile + 2, 4)
    chans, rows, phis, width = bins.shape
    n_chunk = width // LANES
    groups = chans * rows
    half_rows = groups * HALF

    barrier = pltpu.get_barrier_semaphore()
    for step in range(1, 8):
        pl.semaphore_signal(
            barrier, inc=1, device_id=(lax.rem(slab + step, 8), tile), device_id_type=MESH
        )
    for other in (core_peer, x_peer):
        pl.semaphore_signal(barrier, inc=1, device_id=(slab, other), device_id_type=MESH)
    pl.semaphore_wait(barrier, 9)

    def lanes_of(m):
        return pl.ds(pl.multiple_of(m * LANES, LANES), LANES)

    def halo_up(m):
        return pltpu.make_async_remote_copy(
            src_ref=bins.at[:, pl.ds(rows - 2, 2), :, lanes_of(m)],
            dst_ref=lo.at[:, :, :, lanes_of(m)],
            send_sem=halo_send.at[0, m], recv_sem=halo_recv.at[0, m],
            device_id=(jnp.minimum(slab + 1, 7), tile), device_id_type=MESH,
        )

    def halo_down(m):
        return pltpu.make_async_remote_copy(
            src_ref=bins.at[:, pl.ds(0, 2), :, lanes_of(m)],
            dst_ref=hi.at[:, :, :, lanes_of(m)],
            send_sem=halo_send.at[1, m], recv_sem=halo_recv.at[1, m],
            device_id=(jnp.maximum(slab - 1, 0), tile), device_id_type=MESH,
        )

    up_far = (y == 1) & (z < 3)
    down_far = (y == 0) & (z > 0)
    up_relay = (y == 1) & (z > 0)
    down_relay = (y == 0) & (z < 3)

    def up_detour(m):
        return up_far & (m >= 3 - z)

    def down_detour(m):
        return down_far & (m >= z)

    def up_passes(m):
        return up_relay & (m >= 4 - z)

    def down_passes(m):
        return down_relay & (m >= z + 1)

    def hop(m, start, sem, target):
        return pltpu.make_async_remote_copy(
            src_ref=bins.at[:, pl.ds(start, 2), :, lanes_of(m)],
            dst_ref=relay.at[:, :, :, lanes_of(m)],
            send_sem=halo_send.at[sem, m], recv_sem=relay_recv.at[m],
            device_id=(target, tile), device_id_type=MESH,
        )

    def passed(m, sem, target):
        return pltpu.make_async_remote_copy(
            src_ref=relay.at[:, :, :, lanes_of(m)],
            dst_ref=(lo, hi)[sem].at[:, :, :, lanes_of(m)],
            send_sem=relay_send.at[m], recv_sem=halo_recv.at[sem, m],
            device_id=(target, tile), device_id_type=MESH,
        )

    def hop_up(m):
        return hop(m, rows - 2, 0, jnp.minimum(slab + 2, 7))

    def hop_down(m):
        return hop(m, 0, 1, jnp.maximum(slab - 2, 0))

    def pass_up(m):
        return passed(m, 0, jnp.maximum(slab - 1, 0))

    def pass_down(m):
        return passed(m, 1, jnp.minimum(slab + 1, 7))

    def halo_start(m):
        @pl.when((slab < 7) & jnp.logical_not(up_detour(m)))
        def _():
            halo_up(m).start()

        @pl.when((slab > 0) & jnp.logical_not(down_detour(m)))
        def _():
            halo_down(m).start()

    def hop_start(m):
        @pl.when(up_detour(m))
        def _():
            hop_up(m).start()

        @pl.when(down_detour(m))
        def _():
            hop_down(m).start()

    def relay_pass(m):
        @pl.when(up_passes(m))
        def _():
            hop_up(m).wait_recv()
            pass_up(m).start()

        @pl.when(down_passes(m))
        def _():
            hop_down(m).wait_recv()
            pass_down(m).start()

    for m in range(DEPTH):
        halo_start(m)
    for m in range(1, n_chunk):
        hop_start(m)

    @pl.when(slab == 0)
    def _():
        lo[...] = jnp.zeros_like(lo)

    @pl.when(slab == 7)
    def _():
        hi[...] = jnp.zeros_like(hi)

    for ref in (f0, f1):
        for c in range(ref.shape[0]):
            for t in range(ref.shape[1]):
                ref[c, t, 184:208, :] = jnp.zeros((24, LANES), jnp.float32)

    for m in range(1, DEPTH):
        relay_pass(m)

    def core_copy(m):
        return pltpu.make_async_remote_copy(
            src_ref=smooth.at[:, lanes_of(m)], dst_ref=partner.at[:, lanes_of(m)],
            send_sem=core_send.at[m], recv_sem=core_recv.at[m],
            device_id=(slab, core_peer), device_id_type=MESH,
        )

    def x_copy(m):
        start = pl.multiple_of((1 - chip) * half_rows, HALF)
        return pltpu.make_async_remote_copy(
            src_ref=smooth.at[pl.ds(start, half_rows), lanes_of(m)],
            dst_ref=across.at[:, lanes_of(m)],
            send_sem=x_send.at[m], recv_sem=x_recv.at[m],
            device_id=(slab, x_peer), device_id_type=MESH,
        )

    def sweep(ref, c, e, r, coef):
        here = ref[c, e, pl.ds(OFF + r, HALF), :]
        near = ref[c, e + 1, pl.ds(OFF + r, HALF), :] + ref[c, e - 1, pl.ds(OFF + r, HALF), :]
        if c + 1 < chans:
            near = near + ref[c + 1, e, pl.ds(OFF + r, HALF), :]
        if c > 0:
            near = near + ref[c - 1, e, pl.ds(OFF + r, HALF), :]
        near = near + ref[c, e, pl.ds(OFF + r - 1, HALF), :]
        near = near + ref[c, e, pl.ds(OFF + r + 1, HALF), :]
        return here + coef * (near - 6.0 * here)

    def chunk(m, carry):
        @pl.when(slab > 0)
        def _():
            halo_up(m).wait_recv()

        @pl.when(slab < 7)
        def _():
            halo_down(m).wait_recv()

        @pl.when(slab < 7)
        def _():
            halo_up(m).wait_send()

        @pl.when(slab > 0)
        def _():
            halo_down(m).wait_send()

        @pl.when(m + DEPTH < n_chunk)
        def _():
            halo_start(m + DEPTH)
            relay_pass(m + DEPTH)

        lanes = lanes_of(m)
        for c in range(chans):
            for e in range(rows + 4):
                if e < 2:
                    block = lo[c, e, :, lanes]
                elif e < rows + 2:
                    block = bins[c, e - 2, :, lanes]
                else:
                    block = hi[c, e - rows - 2, :, lanes]
                block = block.astype(jnp.float32)
                f0[c, e, OFF:OFF + phis, :] = block
                f0[c, e, OFF - 1:OFF, :] = block[phis - 1:phis]
                f0[c, e, OFF + phis:OFF + phis + 1, :] = block[0:1]

        def first(t, carry):
            for c in range(chans):
                for r in (0, HALF):
                    f1[c, t, pl.ds(OFF + r, HALF), :] = sweep(
                        f0, c, t + 1, r, diff[c, t, pl.ds(r, HALF), :]
                    )
                f1[c, t, OFF - 1:OFF, :] = f1[c, t, OFF + phis - 1:OFF + phis, :]
                f1[c, t, OFF + phis:OFF + phis + 1, :] = f1[c, t, OFF:OFF + 1, :]
            return carry

        lax.fori_loop(0, rows + 2, first, 0)

        def second(t, carry):
            for c in range(chans):
                for h in range(2):
                    r = h * HALF
                    value = sweep(f1, c, t + 1, r, diff[c, t + 1, pl.ds(r, HALF), :])
                    value = value * mask[t, pl.ds(r, HALF), :]
                    at = pl.multiple_of(h * half_rows + (c * rows + t) * HALF, HALF)
                    smooth[pl.ds(at, HALF), lanes] = value.astype(jnp.bfloat16)
            return carry

        lax.fori_loop(0, rows, second, 0)
        core_copy(m).start()
        x_copy(m).start()
        return carry

    lax.fori_loop(0, n_chunk, chunk, 0)

    def y_copies(k):
        at, size = SEGS[k]
        cols = pl.ds(at, size)
        return [
            pltpu.make_async_remote_copy(
                src_ref=src.at[:, cols] if src.ndim == 2 else src.at[:, :, cols],
                dst_ref=dst.at[:, cols] if src.ndim == 2 else dst.at[:, :, cols],
                send_sem=send.at[k], recv_sem=recv.at[k],
                device_id=(2 * z + 1 - y, tile), device_id_type=MESH,
            )
            for src, dst, send, recv in (
                (yout, ybuf, y_send, y_recv), (youtu, ybufu, yu_send, yu_recv)
            )
        ]

    def z_copies(k, step):
        at, size = SEGS[k]
        cols = pl.ds(at, size)
        zz = lax.rem(z + step, 4)
        return [
            pltpu.make_async_remote_copy(
                src_ref=src.at[step - 1, :, cols], dst_ref=dst.at[step - 1, :, cols],
                send_sem=send.at[k, step - 1], recv_sem=recv.at[k, step - 1],
                device_id=(2 * zz + y, tile), device_id_type=MESH,
            )
            for src, dst, send, recv in (
                (zout, zbuf, z_send, z_recv), (zoutu, zbufu, zu_send, zu_recv)
            )
        ]

    def gather_copy(k, peer, send, recv):
        at, size = SEGS[k]
        return pltpu.make_async_remote_copy(
            src_ref=out.at[tile, :, pl.ds(at, size)], dst_ref=out.at[tile, :, pl.ds(at, size)],
            send_sem=send.at[k], recv_sem=recv.at[k],
            device_id=(slab, peer), device_id_type=MESH,
        )

    def forward_copy(k):
        at, size = SEGS[k]
        return pltpu.make_async_remote_copy(
            src_ref=out.at[x_peer, :, pl.ds(at, size)], dst_ref=out.at[x_peer, :, pl.ds(at, size)],
            send_sem=gf_send.at[k], recv_sem=gf_recv.at[k],
            device_id=(slab, core_peer), device_id_type=MESH,
        )

    def gram_rows(block):
        return pl.ds(pl.multiple_of(block * 64, 64), 64)

    def y_start(k):
        at, size = SEGS[k]
        cols = pl.ds(at, size)
        for zz in range(4):
            code, unit = coded(gram[gram_rows(2 * zz + 1 - y), cols])
            yout[pl.ds(zz * 64, 64), cols] = code
            youtu[zz, :, cols] = unit
        for copy in y_copies(k):
            copy.start()

    def y_finish(k):
        at, size = SEGS[k]
        cols = pl.ds(at, size)
        for copy in y_copies(k):
            copy.wait_recv()
        for zz in range(4):
            gram[gram_rows(2 * zz + y), cols] += decoded(
                ybuf[pl.ds(zz * 64, 64), cols], ybufu[zz, :, cols]
            )
        for step in (2, 1, 3):
            code, unit = coded(gram[gram_rows(2 * lax.rem(z + step, 4) + y), cols])
            zout[step - 1, :, cols] = code
            zoutu[step - 1, :, cols] = unit
            for copy in z_copies(k, step):
                copy.start()

    def z_finish(k):
        at, size = SEGS[k]
        for step in (1, 2, 3):
            for copy in z_copies(k, step):
                copy.wait_recv()
        cols = pl.ds(at, size)
        total = gram[pl.ds(pl.multiple_of(slab * 64, 64), 64), cols]
        for step in range(3):
            total = total + decoded(zbuf[step, :, cols], zbufu[step, :, cols])
        out[tile, :, cols] = total * scale
        gather_copy(k, x_peer, gx_send, gx_recv).start()
        gather_copy(k, core_peer, g_send, g_recv).start()

    def pair(left, right, at):
        gram[:, at:at + right.shape[1]] = contract(left[...], right[...])

    def half_of(ref, h):
        return ref.at[h * half_rows:(h + 1) * half_rows, :]

    own = slice(0, 512)
    gram[:, own] = contract(half_of(smooth, 0)[...], half_of(smooth, 0)[...])
    gram[:, own] += contract(half_of(smooth, 1)[...], half_of(smooth, 1)[...])
    y_start(0)
    for m in range(n_chunk):
        core_copy(m).wait_recv()
    for c in range(2):
        left, right = (smooth, partner) if c == 0 else (partner, smooth)

        @pl.when(core == c)
        def _():
            cols = slice(c * 256, c * 256 + 256)
            gram[:, 512:768] = contract(left[0:half_rows, :], right[0:half_rows, cols])
            gram[:, 512:768] += contract(left[half_rows:, :], right[half_rows:, cols])
    y_start(1)
    for m in range(n_chunk):
        x_copy(m).wait_recv()
    for piece in range(2):
        for x in range(2):
            for c in range(2):
                mine = smooth if piece == c else partner

                @pl.when(tile == 2 * x + c)
                def _():
                    if x == 0:
                        pair(half_of(mine, 0), across, 768 + 512 * piece)
                    else:
                        pair(across, half_of(mine, 1), 768 + 512 * piece)
        y_start(2 + piece)
    def forward(k):
        gather_copy(k, x_peer, gx_send, gx_recv).wait_recv()
        forward_copy(k).start()

    y_finish(0)
    y_finish(1)
    z_finish(0)
    y_finish(2)
    z_finish(1)
    y_finish(3)
    forward(0)
    z_finish(2)
    forward(1)
    z_finish(3)
    forward(2)
    forward(3)
    for k in range(4):
        gather_copy(k, core_peer, g_send, g_recv).wait_recv()
        forward_copy(k).wait_recv()

    for m in range(n_chunk):
        @pl.when(up_passes(m))
        def _():
            pass_up(m).wait_send()

        @pl.when(down_passes(m))
        def _():
            pass_down(m).wait_send()
        core_copy(m).wait_send()
        x_copy(m).wait_send()
    for k in range(4):
        for copy in y_copies(k):
            copy.wait_send()
        for step in (1, 2, 3):
            for copy in z_copies(k, step):
                copy.wait_send()
        gather_copy(k, x_peer, gx_send, gx_recv).wait_send()
        gather_copy(k, core_peer, g_send, g_recv).wait_send()
        forward_copy(k).wait_send()


def fused(brdf_bins, diffusion, valid_mask, tile_owner):
    chans, rows, phis, width = brdf_bins.shape
    slab = lax.axis_index("slab")
    my_tile = lax.axis_index("tile")
    margin = jnp.pad(diffusion, ((0, 0), (1, 1), (0, 2 * HALF - phis)))
    local = lax.dynamic_slice_in_dim(margin, slab * rows, rows + 2, 1)
    diff = jnp.broadcast_to(local[..., None], local.shape + (LANES,))
    mask = jnp.pad(valid_mask.astype(jnp.float32), ((0, 0), (0, 2 * HALF - phis)))
    mask = jnp.broadcast_to(mask[..., None], mask.shape + (LANES,))
    scale = 1.0 / math.sqrt(chans * rows * phis * lax.axis_size("slab"))
    dma = pltpu.SemaphoreType.DMA
    all_rows = chans * rows * 2 * HALF
    parts = pl.pallas_call(
        functools.partial(gram_kernel, scale),
        out_shape=jax.ShapeDtypeStruct((4, 64, 1792), jnp.float32),
        in_specs=[pl.BlockSpec(memory_space=pltpu.VMEM)] * 3,
        out_specs=pl.BlockSpec(memory_space=pltpu.VMEM),
        scratch_shapes=[
            pltpu.VMEM((chans, 2, phis, width), jnp.bfloat16),
            pltpu.VMEM((chans, 2, phis, width), jnp.bfloat16),
            pltpu.VMEM((chans, 2, phis, width), jnp.bfloat16),
            pltpu.VMEM((chans, rows + 4, 208, LANES), jnp.float32),
            pltpu.VMEM((chans, rows + 2, 208, LANES), jnp.float32),
            pltpu.VMEM((all_rows, width), jnp.bfloat16),
            pltpu.VMEM((all_rows, width), jnp.bfloat16),
            pltpu.VMEM((all_rows // 2, width), jnp.bfloat16),
            pltpu.VMEM((512, 1792), jnp.float32),
            pltpu.VMEM((256, 1792), jnp.int16),
            pltpu.VMEM((256, 1792), jnp.int16),
            pltpu.VMEM((4, 1, 1792), jnp.float32),
            pltpu.VMEM((4, 1, 1792), jnp.float32),
            pltpu.VMEM((3, 64, 1792), jnp.int16),
            pltpu.VMEM((3, 64, 1792), jnp.int16),
            pltpu.VMEM((3, 1, 1792), jnp.float32),
            pltpu.VMEM((3, 1, 1792), jnp.float32),
            dma((2, 4)), dma((2, 4)), dma((4,)), dma((4,)), dma((4,)), dma((4,)), dma((4,)), dma((4,)),
            dma((4,)), dma((4,)), dma((4,)), dma((4,)),
            dma((4, 3)), dma((4, 3)), dma((4, 3)), dma((4, 3)),
            dma((4,)), dma((4,)), dma((4,)), dma((4,)), dma((4,)), dma((4,)),
        ],
        compiler_params=pltpu.CompilerParams(
            collective_id=0, has_side_effects=True, vmem_limit_bytes=48 * 1024 * 1024
        ),
    )(brdf_bins, diff, mask)
    own = [parts[t, :, 0:512] for t in range(4)]
    side = [parts[t, :, 512:768] for t in range(4)]
    cross = [[parts[t, :, 768 + 512 * p:1280 + 512 * p] for p in range(2)] for t in range(4)]
    row_tile, col_tile = np.triu_indices(4)
    tiles = []
    for i, j in zip(row_tile.tolist(), col_tile.tolist()):
        if i == j:
            tiles.append(own[i])
        elif i // 2 == j // 2:
            tiles.append(jnp.concatenate([side[i], side[j]], axis=1))
        else:
            tiles.append(cross[j - 2][i] + cross[2 + i][j - 2])
    tiles = jnp.stack(tiles)
    n_upper = len(row_tile)
    position = jnp.arange(n_upper, dtype=jnp.int32)
    before = (tile_owner[None, :] == tile_owner[:, None]) & (position[None, :] < position[:, None])
    rank_in = jnp.sum(before.astype(jnp.int32), axis=1)
    cap_slots = 2 * ((n_upper + 3) // 4)
    slot_ids = jnp.arange(cap_slots, dtype=jnp.int32)
    chosen = (tile_owner[None, :] == my_tile) & (rank_in[None, :] == slot_ids[:, None])
    source = jnp.sum(jnp.where(chosen, position[None, :], 0), axis=1).astype(jnp.int32)
    picked = jnp.take(tiles, source, axis=0)
    return jnp.where(jnp.any(chosen, axis=1)[:, None, None], picked, 0.0)


def solution(mesh):
    body = fused if (mesh.shape["slab"], mesh.shape["tile"]) == (8, 4) else on_device
    in_specs = (P(None, "slab", None, "tile"), P(), P("slab", None), P())
    out_specs = P("tile", "slab", None)
    return jax.shard_map(
        body, mesh=mesh, in_specs=in_specs, out_specs=out_specs, check_vma=False
    )
```

```python
import functools
import math

import jax
import jax.numpy as jnp
import numpy as np
from jax import lax
from jax.experimental import pallas as pl
from jax.experimental.pallas import tpu as pltpu
from jax.sharding import PartitionSpec as P

SWEEPS = 2


def padded_2(cells, sides, width):
    for axis, dim in sides:
        count = lax.axis_size(axis)
        ends = count - 1
        head = lax.slice_in_dim(cells, 0, width, axis=dim)
        tail = lax.slice_in_dim(cells, cells.shape[dim] - width, cells.shape[dim], axis=dim)
        cells = jnp.concatenate(
            [
                lax.ppermute(tail, axis, [(i, (i + 1) % count) for i in range(ends)]),
                cells,
                lax.ppermute(head, axis, [((i + 1) % count, i) for i in range(ends)]),
            ],
            axis=dim,
        )
    return cells


def stencil(padded, diffusion_rows):
    center = padded[:, 1:-1]
    pad_chan = jnp.pad(center, ((1, 1), (0, 0), (0, 0), (0, 0)))
    neighbours = padded[:, 2:] + padded[:, :-2] + pad_chan[2:] + pad_chan[:-2]
    neighbours = neighbours + jnp.roll(center, 1, 2) + jnp.roll(center, -1, 2)
    return center + diffusion_rows[..., None] * (neighbours - 6.0 * center)


def contract_rows(left_cols, right_cols):
    return lax.dot_general(
        left_cols, right_cols, (((0,), (0,)), ((), ())), preferred_element_type=jnp.float32
    )


def on_device(brdf_bins, diffusion, valid_mask, tile_owner):
    n_tiles = lax.axis_size("tile")
    my_tile = lax.axis_index("tile")
    slab_width = brdf_bins.shape[1]
    slab_start = lax.axis_index("slab") * slab_width
    extended = padded_2(brdf_bins, (("slab", 1),), SWEEPS)
    field = extended.astype(jnp.float32)
    margin_diffusion = jnp.pad(diffusion, ((0, 0), (SWEEPS - 1, SWEEPS - 1), (0, 0)))
    for sweep_idx in range(SWEEPS):
        span_rows = slab_width + 2 * (SWEEPS - 1 - sweep_idx)
        local_diffusion = lax.dynamic_slice_in_dim(
            margin_diffusion, slab_start + sweep_idx, span_rows, 1
        )
        field = stencil(field, local_diffusion)
    smooth = (field * valid_mask[None, :, :, None].astype(jnp.float32)).astype(jnp.bfloat16)
    flat_rows = smooth.reshape(-1, smooth.shape[-1])
    tile_width = flat_rows.shape[1]
    gram_scale = 1.0 / math.sqrt(flat_rows.shape[0] * lax.axis_size("slab"))
    row_tile, col_tile = np.triu_indices(n_tiles)
    n_upper = row_tile.shape[0]
    column_block = contract_rows(lax.all_gather(flat_rows, "tile", axis=1, tiled=True), flat_rows)
    tile_slots = column_block.reshape(n_tiles, tile_width, tile_width)
    slot_table = np.full((n_tiles, n_tiles), -1, np.int32)
    slot_table[col_tile, row_tile] = np.arange(n_upper, dtype=np.int32)
    reduced = lax.psum_scatter(tile_slots, "slab", scatter_dimension=1, tiled=True) * gram_scale
    my_upper = jnp.asarray(slot_table)[my_tile]
    has_upper = my_upper >= 0
    safe_upper = jnp.clip(my_upper, 0, n_upper - 1)
    destination = jnp.where(has_upper, tile_owner[safe_upper], -1)
    position = jnp.arange(n_upper, dtype=jnp.int32)
    same_owner = tile_owner[None, :] == tile_owner[:, None]
    before = same_owner & (position[None, :] < position[:, None])
    rank_in = jnp.sum(before.astype(jnp.int32), axis=1)
    to_dest = (destination[None, :] == jnp.arange(n_tiles, dtype=jnp.int32)[:, None]).astype(
        jnp.float32
    )
    outgoing = to_dest[:, :, None, None] * reduced[None]
    received = lax.all_to_all(outgoing, "tile", split_axis=0, concat_axis=0, tiled=True)
    received = received.reshape(n_tiles * n_tiles, received.shape[2], received.shape[3])
    recv_index = jnp.asarray((col_tile * n_tiles + row_tile).astype(np.int32))
    cap_slots = 2 * ((n_upper + n_tiles - 1) // n_tiles)
    slot_ids = jnp.arange(cap_slots, dtype=jnp.int32)
    chosen = (tile_owner[None, :] == my_tile) & (rank_in[None, :] == slot_ids[:, None])
    source_idx = jnp.sum(jnp.where(chosen, recv_index[None, :], 0), axis=1).astype(jnp.int32)
    filled = jnp.any(chosen, axis=1)
    picked = jnp.take(received, source_idx, axis=0)
    return jnp.where(filled[:, None, None], picked, 0.0)


MESH = pl.DeviceIdType.MESH
LANES = 128
HALF = 96
OFF = 8
DEPTH = 2
LEVELS = 32767.0
SEGS = ((0, 512), (512, 256), (768, 512), (1280, 512))


def contract(left, right):
    return lax.dot_general(
        left, right, (((0,), (0,)), ((), ())), preferred_element_type=jnp.float32
    )


def coded(block):
    peak = jnp.maximum(jnp.max(jnp.abs(block), axis=0, keepdims=True), 1e-30)
    code = jnp.round(block * (LEVELS / peak)).astype(jnp.int32).astype(jnp.int16)
    return code, peak * (1.0 / LEVELS)


def decoded(code, unit):
    return code.astype(jnp.int32).astype(jnp.float32) * unit


def gram_kernel(
    scale, bins, diff, mask, out, lo, hi, relay, f0, f1, smooth, partner, across, gram,
    yout, ybuf, youtu, ybufu, zout, zbuf, zoutu, zbufu, gcode, gunit,
    halo_send, halo_recv, relay_send, relay_recv, core_send, core_recv, x_send, x_recv, y_send, y_recv, yu_send, yu_recv,
    z_send, z_recv, zu_send, zu_recv,
    g_send, g_recv, gx_send, gx_recv, gf_send, gf_recv,
    gu_send, gu_recv, gxu_send, gxu_recv, gfu_send, gfu_recv,
):
    slab = lax.axis_index("slab")
    tile = lax.axis_index("tile")
    z = slab // 2
    y = lax.rem(slab, 2)
    chip = tile // 2
    core = lax.rem(tile, 2)
    core_peer = 2 * chip + 1 - core
    x_peer = lax.rem(tile + 2, 4)
    chans, rows, phis, width = bins.shape
    n_chunk = width // LANES
    groups = chans * rows
    half_rows = groups * HALF

    barrier = pltpu.get_barrier_semaphore()
    for step in range(1, 8):
        pl.semaphore_signal(
            barrier, inc=1, device_id=(lax.rem(slab + step, 8), tile), device_id_type=MESH
        )
    for other in (core_peer, x_peer):
        pl.semaphore_signal(barrier, inc=1, device_id=(slab, other), device_id_type=MESH)
    pl.semaphore_wait(barrier, 9)

    def lanes_of(m):
        return pl.ds(pl.multiple_of(m * LANES, LANES), LANES)

    def halo_up(m):
        return pltpu.make_async_remote_copy(
            src_ref=bins.at[:, pl.ds(rows - 2, 2), :, lanes_of(m)],
            dst_ref=lo.at[:, :, :, lanes_of(m)],
            send_sem=halo_send.at[0, m], recv_sem=halo_recv.at[0, m],
            device_id=(jnp.minimum(slab + 1, 7), tile), device_id_type=MESH,
        )

    def halo_down(m):
        return pltpu.make_async_remote_copy(
            src_ref=bins.at[:, pl.ds(0, 2), :, lanes_of(m)],
            dst_ref=hi.at[:, :, :, lanes_of(m)],
            send_sem=halo_send.at[1, m], recv_sem=halo_recv.at[1, m],
            device_id=(jnp.maximum(slab - 1, 0), tile), device_id_type=MESH,
        )

    up_far = (y == 1) & (z < 3)
    down_far = (y == 0) & (z > 0)
    up_relay = (y == 1) & (z > 0)
    down_relay = (y == 0) & (z < 3)

    def up_detour(m):
        return up_far & (m >= 3 - z)

    def down_detour(m):
        return down_far & (m >= z)

    def up_passes(m):
        return up_relay & (m >= 4 - z)

    def down_passes(m):
        return down_relay & (m >= z + 1)

    def hop(m, start, sem, target):
        return pltpu.make_async_remote_copy(
            src_ref=bins.at[:, pl.ds(start, 2), :, lanes_of(m)],
            dst_ref=relay.at[:, :, :, lanes_of(m)],
            send_sem=halo_send.at[sem, m], recv_sem=relay_recv.at[m],
            device_id=(target, tile), device_id_type=MESH,
        )

    def passed(m, sem, target):
        return pltpu.make_async_remote_copy(
            src_ref=relay.at[:, :, :, lanes_of(m)],
            dst_ref=(lo, hi)[sem].at[:, :, :, lanes_of(m)],
            send_sem=relay_send.at[m], recv_sem=halo_recv.at[sem, m],
            device_id=(target, tile), device_id_type=MESH,
        )

    def hop_up(m):
        return hop(m, rows - 2, 0, jnp.minimum(slab + 2, 7))

    def hop_down(m):
        return hop(m, 0, 1, jnp.maximum(slab - 2, 0))

    def pass_up(m):
        return passed(m, 0, jnp.maximum(slab - 1, 0))

    def pass_down(m):
        return passed(m, 1, jnp.minimum(slab + 1, 7))

    def halo_start(m):
        @pl.when((slab < 7) & jnp.logical_not(up_detour(m)))
        def _():
            halo_up(m).start()

        @pl.when((slab > 0) & jnp.logical_not(down_detour(m)))
        def _():
            halo_down(m).start()

    def hop_start(m):
        @pl.when(up_detour(m))
        def _():
            hop_up(m).start()

        @pl.when(down_detour(m))
        def _():
            hop_down(m).start()

    def relay_pass(m):
        @pl.when(up_passes(m))
        def _():
            hop_up(m).wait_recv()
            pass_up(m).start()

        @pl.when(down_passes(m))
        def _():
            hop_down(m).wait_recv()
            pass_down(m).start()

    for m in range(DEPTH):
        halo_start(m)
    for m in range(1, n_chunk):
        hop_start(m)

    @pl.when(slab == 0)
    def _():
        lo[...] = jnp.zeros_like(lo)

    @pl.when(slab == 7)
    def _():
        hi[...] = jnp.zeros_like(hi)

    for ref in (f0, f1):
        for c in range(ref.shape[0]):
            for t in range(ref.shape[1]):
                ref[c, t, 184:208, :] = jnp.zeros((24, LANES), jnp.float32)

    for m in range(1, DEPTH):
        relay_pass(m)

    def core_copy(m):
        return pltpu.make_async_remote_copy(
            src_ref=smooth.at[:, lanes_of(m)], dst_ref=partner.at[:, lanes_of(m)],
            send_sem=core_send.at[m], recv_sem=core_recv.at[m],
            device_id=(slab, core_peer), device_id_type=MESH,
        )

    def x_copy(m):
        start = pl.multiple_of((1 - chip) * half_rows, HALF)
        return pltpu.make_async_remote_copy(
            src_ref=smooth.at[pl.ds(start, half_rows), lanes_of(m)],
            dst_ref=across.at[:, lanes_of(m)],
            send_sem=x_send.at[m], recv_sem=x_recv.at[m],
            device_id=(slab, x_peer), device_id_type=MESH,
        )

    def sweep(ref, c, e, r, coef):
        here = ref[c, e, pl.ds(OFF + r, HALF), :]
        near = ref[c, e + 1, pl.ds(OFF + r, HALF), :] + ref[c, e - 1, pl.ds(OFF + r, HALF), :]
        if c + 1 < chans:
            near = near + ref[c + 1, e, pl.ds(OFF + r, HALF), :]
        if c > 0:
            near = near + ref[c - 1, e, pl.ds(OFF + r, HALF), :]
        near = near + ref[c, e, pl.ds(OFF + r - 1, HALF), :]
        near = near + ref[c, e, pl.ds(OFF + r + 1, HALF), :]
        return here + coef * (near - 6.0 * here)

    def chunk(m, carry):
        @pl.when(slab > 0)
        def _():
            halo_up(m).wait_recv()

        @pl.when(slab < 7)
        def _():
            halo_down(m).wait_recv()

        @pl.when(slab < 7)
        def _():
            halo_up(m).wait_send()

        @pl.when(slab > 0)
        def _():
            halo_down(m).wait_send()

        @pl.when(m + DEPTH < n_chunk)
        def _():
            halo_start(m + DEPTH)
            relay_pass(m + DEPTH)

        lanes = lanes_of(m)
        for c in range(chans):
            for e in range(rows + 4):
                if e < 2:
                    block = lo[c, e, :, lanes]
                elif e < rows + 2:
                    block = bins[c, e - 2, :, lanes]
                else:
                    block = hi[c, e - rows - 2, :, lanes]
                block = block.astype(jnp.float32)
                f0[c, e, OFF:OFF + phis, :] = block
                f0[c, e, OFF - 1:OFF, :] = block[phis - 1:phis]
                f0[c, e, OFF + phis:OFF + phis + 1, :] = block[0:1]

        def first(t, carry):
            for c in range(chans):
                for r in (0, HALF):
                    f1[c, t, pl.ds(OFF + r, HALF), :] = sweep(
                        f0, c, t + 1, r, diff[c, t, pl.ds(r, HALF), :]
                    )
                f1[c, t, OFF - 1:OFF, :] = f1[c, t, OFF + phis - 1:OFF + phis, :]
                f1[c, t, OFF + phis:OFF + phis + 1, :] = f1[c, t, OFF:OFF + 1, :]
            return carry

        lax.fori_loop(0, rows + 2, first, 0)

        def second(t, carry):
            for c in range(chans):
                for h in range(2):
                    r = h * HALF
                    value = sweep(f1, c, t + 1, r, diff[c, t + 1, pl.ds(r, HALF), :])
                    value = value * mask[t, pl.ds(r, HALF), :]
                    at = pl.multiple_of(h * half_rows + (c * rows + t) * HALF, HALF)
                    smooth[pl.ds(at, HALF), lanes] = value.astype(jnp.bfloat16)
            return carry

        lax.fori_loop(0, rows, second, 0)
        core_copy(m).start()
        x_copy(m).start()
        return carry

    lax.fori_loop(0, n_chunk, chunk, 0)

    def y_copies(k):
        at, size = SEGS[k]
        cols = pl.ds(at, size)
        return [
            pltpu.make_async_remote_copy(
                src_ref=src.at[:, cols] if src.ndim == 2 else src.at[:, :, cols],
                dst_ref=dst.at[:, cols] if src.ndim == 2 else dst.at[:, :, cols],
                send_sem=send.at[k], recv_sem=recv.at[k],
                device_id=(2 * z + 1 - y, tile), device_id_type=MESH,
            )
            for src, dst, send, recv in (
                (yout, ybuf, y_send, y_recv), (youtu, ybufu, yu_send, yu_recv)
            )
        ]

    def z_copies(k, step):
        at, size = SEGS[k]
        cols = pl.ds(at, size)
        zz = lax.rem(z + step, 4)
        return [
            pltpu.make_async_remote_copy(
                src_ref=src.at[step - 1, :, cols], dst_ref=dst.at[step - 1, :, cols],
                send_sem=send.at[k, step - 1], recv_sem=recv.at[k, step - 1],
                device_id=(2 * zz + y, tile), device_id_type=MESH,
            )
            for src, dst, send, recv in (
                (zout, zbuf, z_send, z_recv), (zoutu, zbufu, zu_send, zu_recv)
            )
        ]

    def shared(k, source, peer, sems):
        at, size = SEGS[k]
        cols = pl.ds(at, size)
        return [
            pltpu.make_async_remote_copy(
                src_ref=ref.at[source, :, cols], dst_ref=ref.at[source, :, cols],
                send_sem=sems[2 * n].at[k], recv_sem=sems[2 * n + 1].at[k],
                device_id=(slab, peer), device_id_type=MESH,
            )
            for n, ref in enumerate((gcode, gunit))
        ]

    core_sems = (g_send, g_recv, gu_send, gu_recv)
    across_sems = (gx_send, gx_recv, gxu_send, gxu_recv)
    forward_sems = (gf_send, gf_recv, gfu_send, gfu_recv)

    def gathers(k):
        return shared(k, tile, x_peer, across_sems) + shared(k, tile, core_peer, core_sems)

    def forwards(k):
        return shared(k, x_peer, core_peer, forward_sems)

    def decode_from(k, source):
        at, size = SEGS[k]
        cols = pl.ds(at, size)
        out[source, :, cols] = decoded(gcode[source, :, cols], gunit[source, :, cols])

    def gram_rows(block):
        return pl.ds(pl.multiple_of(block * 64, 64), 64)

    def y_start(k):
        at, size = SEGS[k]
        cols = pl.ds(at, size)
        for zz in range(4):
            code, unit = coded(gram[gram_rows(2 * zz + 1 - y), cols])
            yout[pl.ds(zz * 64, 64), cols] = code
            youtu[zz, :, cols] = unit
        for copy in y_copies(k):
            copy.start()

    def y_finish(k):
        at, size = SEGS[k]
        cols = pl.ds(at, size)
        for copy in y_copies(k):
            copy.wait_recv()
        for zz in range(4):
            gram[gram_rows(2 * zz + y), cols] += decoded(
                ybuf[pl.ds(zz * 64, 64), cols], ybufu[zz, :, cols]
            )
        for step in (2, 1, 3):
            code, unit = coded(gram[gram_rows(2 * lax.rem(z + step, 4) + y), cols])
            zout[step - 1, :, cols] = code
            zoutu[step - 1, :, cols] = unit
            for copy in z_copies(k, step):
                copy.start()

    def z_finish(k):
        at, size = SEGS[k]
        for step in (1, 2, 3):
            for copy in z_copies(k, step):
                copy.wait_recv()
        cols = pl.ds(at, size)
        total = gram[pl.ds(pl.multiple_of(slab * 64, 64), 64), cols]
        for step in range(3):
            total = total + decoded(zbuf[step, :, cols], zbufu[step, :, cols])
        total = total * scale
        code, unit = coded(total)
        gcode[tile, :, cols] = code
        gunit[tile, :, cols] = unit
        for copy in gathers(k):
            copy.start()
        out[tile, :, cols] = total

    def pair(left, right, at):
        gram[:, at:at + right.shape[1]] = contract(left[...], right[...])

    def half_of(ref, h):
        return ref.at[h * half_rows:(h + 1) * half_rows, :]

    own = slice(0, 512)
    gram[:, own] = contract(half_of(smooth, 0)[...], half_of(smooth, 0)[...])
    gram[:, own] += contract(half_of(smooth, 1)[...], half_of(smooth, 1)[...])
    y_start(0)
    for m in range(n_chunk):
        core_copy(m).wait_recv()
    for c in range(2):
        left, right = (smooth, partner) if c == 0 else (partner, smooth)

        @pl.when(core == c)
        def _():
            cols = slice(c * 256, c * 256 + 256)
            gram[:, 512:768] = contract(left[0:half_rows, :], right[0:half_rows, cols])
            gram[:, 512:768] += contract(left[half_rows:, :], right[half_rows:, cols])
    y_start(1)
    for m in range(n_chunk):
        x_copy(m).wait_recv()
    for piece in range(2):
        for x in range(2):
            for c in range(2):
                mine = smooth if piece == c else partner

                @pl.when(tile == 2 * x + c)
                def _():
                    if x == 0:
                        pair(half_of(mine, 0), across, 768 + 512 * piece)
                    else:
                        pair(across, half_of(mine, 1), 768 + 512 * piece)
        y_start(2 + piece)
    def forward(k):
        for copy in shared(k, tile, x_peer, across_sems):
            copy.wait_recv()
        for copy in forwards(k):
            copy.start()
        decode_from(k, x_peer)

    y_finish(0)
    y_finish(1)
    z_finish(0)
    y_finish(2)
    z_finish(1)
    y_finish(3)
    forward(0)
    z_finish(2)
    forward(1)
    z_finish(3)
    forward(2)
    forward(3)
    for k in range(4):
        for copy in shared(k, tile, core_peer, core_sems):
            copy.wait_recv()
        decode_from(k, core_peer)
    for k in range(4):
        for copy in forwards(k):
            copy.wait_recv()
        decode_from(k, lax.rem(core_peer + 2, 4))

    for m in range(n_chunk):
        @pl.when(up_passes(m))
        def _():
            pass_up(m).wait_send()

        @pl.when(down_passes(m))
        def _():
            pass_down(m).wait_send()
        core_copy(m).wait_send()
        x_copy(m).wait_send()
    for k in range(4):
        for copy in y_copies(k):
            copy.wait_send()
        for step in (1, 2, 3):
            for copy in z_copies(k, step):
                copy.wait_send()
        for copy in gathers(k) + forwards(k):
            copy.wait_send()


def fused(brdf_bins, diffusion, valid_mask, tile_owner):
    chans, rows, phis, width = brdf_bins.shape
    slab = lax.axis_index("slab")
    my_tile = lax.axis_index("tile")
    margin = jnp.pad(diffusion, ((0, 0), (1, 1), (0, 2 * HALF - phis)))
    local = lax.dynamic_slice_in_dim(margin, slab * rows, rows + 2, 1)
    diff = jnp.broadcast_to(local[..., None], local.shape + (LANES,))
    mask = jnp.pad(valid_mask.astype(jnp.float32), ((0, 0), (0, 2 * HALF - phis)))
    mask = jnp.broadcast_to(mask[..., None], mask.shape + (LANES,))
    scale = 1.0 / math.sqrt(chans * rows * phis * lax.axis_size("slab"))
    dma = pltpu.SemaphoreType.DMA
    all_rows = chans * rows * 2 * HALF
    parts = pl.pallas_call(
        functools.partial(gram_kernel, scale),
        out_shape=jax.ShapeDtypeStruct((4, 64, 1792), jnp.float32),
        in_specs=[pl.BlockSpec(memory_space=pltpu.VMEM)] * 3,
        out_specs=pl.BlockSpec(memory_space=pltpu.VMEM),
        scratch_shapes=[
            pltpu.VMEM((chans, 2, phis, width), jnp.bfloat16),
            pltpu.VMEM((chans, 2, phis, width), jnp.bfloat16),
            pltpu.VMEM((chans, 2, phis, width), jnp.bfloat16),
            pltpu.VMEM((chans, rows + 4, 208, LANES), jnp.float32),
            pltpu.VMEM((chans, rows + 2, 208, LANES), jnp.float32),
            pltpu.VMEM((all_rows, width), jnp.bfloat16),
            pltpu.VMEM((all_rows, width), jnp.bfloat16),
            pltpu.VMEM((all_rows // 2, width), jnp.bfloat16),
            pltpu.VMEM((512, 1792), jnp.float32),
            pltpu.VMEM((256, 1792), jnp.int16),
            pltpu.VMEM((256, 1792), jnp.int16),
            pltpu.VMEM((4, 1, 1792), jnp.float32),
            pltpu.VMEM((4, 1, 1792), jnp.float32),
            pltpu.VMEM((3, 64, 1792), jnp.int16),
            pltpu.VMEM((3, 64, 1792), jnp.int16),
            pltpu.VMEM((3, 1, 1792), jnp.float32),
            pltpu.VMEM((3, 1, 1792), jnp.float32),
            pltpu.VMEM((4, 64, 1792), jnp.int16),
            pltpu.VMEM((4, 1, 1792), jnp.float32),
            dma((2, 4)), dma((2, 4)), dma((4,)), dma((4,)), dma((4,)), dma((4,)), dma((4,)), dma((4,)),
            dma((4,)), dma((4,)), dma((4,)), dma((4,)),
            dma((4, 3)), dma((4, 3)), dma((4, 3)), dma((4, 3)),
            dma((4,)), dma((4,)), dma((4,)), dma((4,)), dma((4,)), dma((4,)),
            dma((4,)), dma((4,)), dma((4,)), dma((4,)), dma((4,)), dma((4,)),
        ],
        compiler_params=pltpu.CompilerParams(
            collective_id=0, has_side_effects=True, vmem_limit_bytes=48 * 1024 * 1024
        ),
    )(brdf_bins, diff, mask)
    own = [parts[t, :, 0:512] for t in range(4)]
    side = [parts[t, :, 512:768] for t in range(4)]
    cross = [[parts[t, :, 768 + 512 * p:1280 + 512 * p] for p in range(2)] for t in range(4)]
    row_tile, col_tile = np.triu_indices(4)
    tiles = []
    for i, j in zip(row_tile.tolist(), col_tile.tolist()):
        if i == j:
            tiles.append(own[i])
        elif i // 2 == j // 2:
            tiles.append(jnp.concatenate([side[i], side[j]], axis=1))
        else:
            tiles.append(cross[j - 2][i] + cross[2 + i][j - 2])
    tiles = jnp.stack(tiles)
    n_upper = len(row_tile)
    position = jnp.arange(n_upper, dtype=jnp.int32)
    before = (tile_owner[None, :] == tile_owner[:, None]) & (position[None, :] < position[:, None])
    rank_in = jnp.sum(before.astype(jnp.int32), axis=1)
    cap_slots = 2 * ((n_upper + 3) // 4)
    slot_ids = jnp.arange(cap_slots, dtype=jnp.int32)
    chosen = (tile_owner[None, :] == my_tile) & (rank_in[None, :] == slot_ids[:, None])
    source = jnp.sum(jnp.where(chosen, position[None, :], 0), axis=1).astype(jnp.int32)
    picked = jnp.take(tiles, source, axis=0)
    return jnp.where(jnp.any(chosen, axis=1)[:, None, None], picked, 0.0)


def solution(mesh):
    body = fused if (mesh.shape["slab"], mesh.shape["tile"]) == (8, 4) else on_device
    in_specs = (P(None, "slab", None, "tile"), P(), P("slab", None), P())
    out_specs = P("tile", "slab", None)
    return jax.shard_map(
        body, mesh=mesh, in_specs=in_specs, out_specs=out_specs, check_vma=False
    )
```
